512 devices in a mesh: ep: 32 (over z, x_lo), fsdp: 16 (over y, x_hi, core).
Axes of the slice: x: 4 (x_hi: 2, x_lo: 2; x = x_hi * 2 + x_lo), y: 4, z: 16, core: 2. Of those that a mesh axis runs over, the one named last changes fastest.
Arguments:
- tokens: bfloat16 [65536, 2048], P(('ep', 'fsdp')), may hold values from -6 to 6
- cotangent: bfloat16 [65536, 2048], P(('ep', 'fsdp')), may hold values from -1.1953125 to 1.1953125
- bucket: int32 [65536, 1], P(('ep', 'fsdp')), may hold values from 0 to 31; in each aligned block of 128 rows (0 to 127, 128 to 255, ...) at most 5 rows name the same one
- w_gate: bfloat16 [32, 2048, 512], P('ep', 'fsdp'), may hold values from -0.125 to 0.125
- w_up: bfloat16 [32, 2048, 512], P('ep', 'fsdp'), may hold values from -0.125 to 0.125
- w_down: bfloat16 [32, 2048, 512], P('ep', 'fsdp'), may hold values from -0.25 to 0.25
Outputs:
- outputs: bfloat16 [65536, 2048], P(('ep', 'fsdp'))
- input_grad: bfloat16 [65536, 2048], P(('ep', 'fsdp'))
- grad_gate: bfloat16 [32, 2048, 512], P('ep', 'fsdp')
- grad_up: bfloat16 [32, 2048, 512], P('ep', 'fsdp')
- grad_down: bfloat16 [32, 2048, 512], P('ep', 'fsdp')
The draws below stay inside these ranges and needn't reach their ends.
Inputs may be any that keep to these rules, and one draw needn't show every extreme that they name: `bucket`: among the 128 rows of one device no expert is named more than 5 times, and in every draw some device names some expert exactly 5 times.
All inputs are finite; a program needn't handle non-finite values.
Results may differ from the reference program's by a relative error of at most 0.019.
Values may be sent and summed in bfloat16 or wider, within the bound.
No kernel may reach another device: no remote copies, remote signals or barrier semaphores. Data moves between devices by JAX's collectives and lax.ppermute only.
A program may use at most 64 MiB of HBM per device.

```python
import math
import jax
import jax.numpy as jnp
import numpy as np
from jax import lax

D = 2048
FF = 512
TOK_DEV = 128
EXPERT_TOTAL = 32
CAP = 5
TOKENS = 65536
N_EP = 32
N_FSDP = 16


def shard_levels(rng, extent, split, least, largest):
    factor_of = 1.0
    for position, shards_of in split:
        draws = jax.random.uniform(jax.random.fold_in(jax.random.fold_in(rng, 6), position), (shards_of,), jnp.float32, least / len(split), largest / len(split))
        factor_of = factor_of * jnp.repeat(jnp.exp(draws), extent[position] // shards_of).reshape((-1,) + (1,) * (len(extent) - 1 - position))
    return factor_of


def assign_block(own_key, own, number, rows, count, top, limit, skew):
    order = jax.random.permutation(own_key, count)
    packed, ordinary = portions_of(count, rows * top, limit, skew, True), portions_of(count, rows * top, limit, skew, False)
    places = jnp.arange(count)

    def named(lengths, rotation):
        used = int((lengths > 0).sum())
        fixed = max(1, used // 4)
        shifted = fixed + (places - fixed + rotation * (used - fixed)) % max(1, count - fixed)
        return jnp.zeros((count,), jnp.int32).at[order[jnp.where(places < fixed, places, shifted)]].set(jnp.asarray(lengths, jnp.int32))

    lengths = jnp.where(number % 4 == 0, named(packed, number // 4), named(ordinary, number - number // 4 - 1))
    mixed = jax.random.permutation(jax.random.fold_in(own, 3), count)
    donor, sink = mixed[0:count // 2 * 2:2], mixed[1:count // 2 * 2:2]
    room = jnp.minimum(lengths[donor] - 1, limit - lengths[sink]) // 2
    room = jnp.where((donor == order[0]) | (sink == order[0]) | (lengths[sink] == 0), 0, jnp.maximum(room, 0))
    shifted = jax.random.randint(jax.random.fold_in(own, 4), (count // 2,), 0, 1 << 20) % (room + 1)
    lengths = lengths.at[donor].add(-shifted).at[sink].add(shifted)
    items = jnp.searchsorted(jnp.cumsum(lengths), jnp.arange(rows * top), side="right").astype(jnp.int32)
    grid = items.reshape(top, rows).T
    grid = grid[jax.random.permutation(jax.random.fold_in(own, 1), rows)]
    rotation = jax.random.randint(jax.random.fold_in(own, 2), (rows, 1), 0, top)
    return jnp.take_along_axis(grid, (jnp.arange(top)[None, :] + rotation) % top, axis=1)


def portions_of(count, total, limit, skew, full):
    portions = [(1 << 20) // math.isqrt(standing ** skew) + 1 for standing in range(1, count + 1)]
    largest = limit if full else min(limit, max(-(-total // count), total * portions[0] // sum(portions)))
    least = 1 if total - largest >= count - 1 else 0
    holding, surplus = [largest] + [least] * (count - 1), total - largest - least * (count - 1)
    while surplus > 0:
        candidates = [i for i in range(1, count) if holding[i] < largest] or [i for i in range(1, count) if holding[i] < limit]
        pool, remaining = sum([portions[i] for i in candidates]), surplus
        for i in candidates:
            more = min(limit - holding[i], max(1, remaining * portions[i] // pool), surplus)
            holding[i] = holding[i] + more
            surplus = surplus - more
    return np.array(holding)


def centred(rng, extent, width, most, pieces=(), kind=jnp.bfloat16):
    array = jax.random.normal(rng, extent, jnp.float32) * width
    if len(pieces) > 0:
        array = shard_levels(rng, extent, pieces, -0.22, 0.18) * array
    return jnp.clip(array, min=-most, max=most).astype(kind)


def setup_inputs(seed: int = 0) -> dict:
    streams_of = jax.random.split(jax.random.key(seed), 7)
    tokens = centred(streams_of[0], (TOKENS, D), 1.0, 6.0, ((0, 512),))
    cotangent = centred(streams_of[1], (TOKENS, D), 0.2, 1.1953125, ((0, 512),))
    bucket_keys = jax.random.split(jax.random.fold_in(streams_of[2], 1), TOKENS // TOK_DEV)
    bucket_turns = jax.random.permutation(jax.random.fold_in(streams_of[2], 3), TOKENS // TOK_DEV)
    bucket = jax.vmap(lambda own, number: assign_block(jax.random.fold_in(streams_of[2], 2), own, number, TOK_DEV, EXPERT_TOTAL, 1, CAP, 1))(bucket_keys, bucket_turns).reshape((TOKENS, 1))
    w_gate = centred(streams_of[3], (EXPERT_TOTAL, D, FF), D ** -0.5, 0.125, ((0, 32), (1, 16)))
    w_up = centred(streams_of[4], (EXPERT_TOTAL, D, FF), D ** -0.5, 0.125, ((0, 32), (1, 16)))
    w_down = centred(streams_of[5], (EXPERT_TOTAL, D, FF), FF ** -0.5, 0.25, ((0, 32), (1, 16)))
    return dict(tokens=tokens, cotangent=cotangent, bucket=bucket, w_gate=w_gate, w_up=w_up, w_down=w_down)


def partial_sum_value(left_rows, right_rows):
    partial_terms = jnp.einsum('fra,frb->fab', left_rows.astype(jnp.float32), right_rows.astype(jnp.float32))
    rounded = lax.optimization_barrier(partial_terms.astype(jnp.bfloat16))
    return jnp.sum(rounded.astype(jnp.float32), axis=0).astype(jnp.bfloat16)


def reference(tokens, cotangent, bucket, w_gate, w_up, w_down):
    device_count = N_EP * N_FSDP
    blocks = bucket[:, 0].reshape(device_count, TOK_DEV)
    labels = jnp.arange(EXPERT_TOTAL, dtype=jnp.int32)
    chosen = (blocks[:, :, None] == labels[None, None, :]).astype(jnp.int32)
    earlier = jnp.cumsum(chosen, axis=1).astype(jnp.int32) - chosen
    slot_index = jnp.sum(earlier * chosen, axis=2).astype(jnp.int32)
    device_ids = jnp.arange(device_count, dtype=jnp.int32)[:, None] * jnp.ones((1, TOK_DEV), jnp.int32)
    source_ep = (device_ids // N_FSDP).astype(jnp.int32)
    source_fsdp = (device_ids % N_FSDP).astype(jnp.int32)
    token_ids = (device_ids * TOK_DEV + jnp.arange(TOK_DEV, dtype=jnp.int32)[None, :]).astype(jnp.int32)
    slot_table = jnp.full((EXPERT_TOTAL, N_FSDP, N_EP, CAP), TOKENS, jnp.int32)
    slot_table = slot_table.at[blocks, source_fsdp, source_ep, slot_index].set(token_ids)
    slot_table = slot_table.reshape(EXPERT_TOTAL, N_FSDP, N_EP * CAP)
    padded_x = jnp.concatenate([tokens, jnp.zeros((1, D), tokens.dtype)], axis=0)
    padded_dy = jnp.concatenate([cotangent, jnp.zeros((1, D), cotangent.dtype)], axis=0)

    def expert_pass(operands):
        rows_table, gate_matrix, up_matrix, down_weight_matrix = operands
        rows_x = padded_x[rows_table]
        rows_dy = padded_dy[rows_table]
        gate_f = gate_matrix.astype(jnp.float32)
        up_f = up_matrix.astype(jnp.float32)
        down_f = down_weight_matrix.astype(jnp.float32)
        gate_pre = jnp.einsum('frd,dj->frj', rows_x.astype(jnp.float32), gate_f)
        up_projection_weight = jnp.einsum('frd,dj->frj', rows_x.astype(jnp.float32), up_f)
        sigmoid_gate = jax.nn.sigmoid(gate_pre)
        activated = gate_pre * sigmoid_gate
        hidden = (activated * up_projection_weight).astype(jnp.bfloat16)
        rows_y = jnp.einsum('frj,dj->frd', hidden.astype(jnp.float32), down_f).astype(jnp.bfloat16)
        grad_hidden = jnp.einsum('frd,dj->frj', rows_dy.astype(jnp.float32), down_f)
        grad_pre_gate = (grad_hidden * up_projection_weight * sigmoid_gate * (1.0 + gate_pre * (1.0 - sigmoid_gate))).astype(jnp.bfloat16)
        grad_pre_up = (grad_hidden * activated).astype(jnp.bfloat16)
        rows_dx = (jnp.einsum('frj,dj->frd', grad_pre_gate.astype(jnp.float32), gate_f)
                   + jnp.einsum('frj,dj->frd', grad_pre_up.astype(jnp.float32), up_f)).astype(jnp.bfloat16)
        grad_wg = partial_sum_value(rows_x, grad_pre_gate)
        grad_wu = partial_sum_value(rows_x, grad_pre_up)
        grad_wd = partial_sum_value(rows_dy, hidden)
        return rows_y, rows_dx, grad_wg, grad_wu, grad_wd

    rows_y, rows_dx, grad_wg, grad_wu, grad_wd = lax.map(expert_pass, (slot_table, w_gate, w_up, w_down))
    flat_table = slot_table.reshape(-1)
    outputs = jnp.zeros((TOKENS + 1, D), jnp.bfloat16).at[flat_table].set(rows_y.reshape(-1, D))[:TOKENS]
    input_grad = jnp.zeros((TOKENS + 1, D), jnp.bfloat16).at[flat_table].set(rows_dx.reshape(-1, D))[:TOKENS]
    return outputs, input_grad, grad_wg, grad_wu, grad_wd
```

```python
import jax
import jax.numpy as jnp
from jax import lax
from jax.sharding import PartitionSpec as P


def slot_matrix(bucket, expert_count, capacity):
    token_count = bucket.shape[0]
    labels = lax.broadcasted_iota(jnp.int32, (token_count, expert_count), 1)
    chosen = (bucket == labels).astype(jnp.int32)
    earlier = jnp.cumsum(chosen, axis=0) - chosen
    slot_index = jnp.sum(earlier * chosen, axis=1)
    position = bucket[:, 0] * capacity + slot_index
    targets = lax.broadcasted_iota(jnp.int32, (expert_count * capacity, token_count), 0)
    return (targets == position[None, :]).astype(jnp.bfloat16)


def contract_rows(left_rows, right_rows):
    return lax.dot_general(
        left_rows, right_rows, (((0,), (0,)), ((), ())), preferred_element_type=jnp.float32
    )


def contract_cols(left_rows, right_rows):
    return lax.dot_general(
        left_rows, right_rows, (((1,), (1,)), ((), ())), preferred_element_type=jnp.float32
    )


def exchange(rows, expert_count):
    row_count, width = rows.shape
    chunk = row_count // expert_count * (width // 128)
    sent = rows.reshape(row_count, width // 128, 128).reshape(expert_count, chunk, 128)
    arrived = lax.all_to_all(sent, "ep", split_axis=0, concat_axis=0, tiled=True)
    return arrived.reshape(row_count, width // 128, 128).reshape(row_count, width)


Y, X_HI = 4, 2


def core_swap(array):
    return lax.ppermute(array, "fsdp", [(f, f ^ 1) for f in range(2 * Y * X_HI)])


def chip_shift(array, dy, dx):
    pairs = []
    for y in range(Y):
        for x in range(X_HI):
            for core in range(2):
                pairs.append(
                    ((y * X_HI + x) * 2 + core, ((y + dy) % Y * X_HI + (x ^ dx)) * 2 + core)
                )
    return lax.ppermute(array, "fsdp", pairs)


def local(tokens, cotangent, bucket, w_gate, w_up, w_down):
    token_count = tokens.shape[0]
    model_width = tokens.shape[1]
    expert_count = lax.axis_size("ep")
    capacity = max(2, 5 * token_count // (4 * expert_count))
    slot_rows = expert_count * capacity
    shard_width = w_gate.shape[1]
    hidden_width = w_gate.shape[2]
    chips = Y * X_HI
    place = lax.axis_index("fsdp")
    core = place % 2
    chip = place // 2

    weights = lax.all_gather(
        jnp.concatenate([w_gate[0], w_up[0], w_down[0]], axis=1), "fsdp", axis=0, tiled=True
    )
    selector = slot_matrix(bucket, expert_count, capacity)
    joined = jnp.concatenate([tokens, cotangent], axis=1)
    packed = jnp.dot(selector, joined, preferred_element_type=jnp.float32).astype(jnp.bfloat16)
    arrived = exchange(packed, expert_count)
    rows_x = arrived[:, :model_width]
    rows_dy = arrived[:, model_width:]

    blocks = arrived.reshape(slot_rows, 2 * chips, 2, shard_width)
    own = jnp.where(core == 0, blocks[:, :, 0], blocks[:, :, 1])
    other = core_swap(jnp.where(core == 0, blocks[:, :, 1], blocks[:, :, 0]))

    w_gate_up = weights[:, : 2 * hidden_width]
    w_out = weights[:, 2 * hidden_width :]
    pre = jnp.dot(rows_x, w_gate_up, preferred_element_type=jnp.float32)
    gate_pre = pre[:, :hidden_width]
    up_proj = pre[:, hidden_width:]
    sigmoid_gate = jax.nn.sigmoid(gate_pre)
    activated = gate_pre * sigmoid_gate
    hidden = (activated * up_proj).astype(jnp.bfloat16)
    rows_y = contract_cols(hidden, w_out).astype(jnp.bfloat16)
    back_y = exchange(rows_y, expert_count)
    grad_hidden = jnp.dot(rows_dy, w_out, preferred_element_type=jnp.float32)
    grad_pre_gate = (
        grad_hidden * up_proj * sigmoid_gate * (1.0 + gate_pre * (1.0 - sigmoid_gate))
    ).astype(jnp.bfloat16)
    grad_pre_up = (grad_hidden * activated).astype(jnp.bfloat16)
    grads_pre = jnp.concatenate([grad_pre_gate, grad_pre_up], axis=1)
    rows_dx = contract_cols(grads_pre, w_gate_up).astype(jnp.bfloat16)
    back_dx = exchange(rows_dx, expert_count)

    sides = jnp.concatenate([grads_pre, hidden], axis=1)
    other_sides = core_swap(sides)
    pair_rows = jnp.concatenate([own, other], axis=0)
    pair_sides = jnp.concatenate([sides, other_sides], axis=0)

    def terms(target):
        x_block = lax.dynamic_index_in_dim(pair_rows, target, 1, keepdims=False)
        dy_block = lax.dynamic_index_in_dim(pair_rows, target + chips, 1, keepdims=False)
        gate_up = contract_rows(x_block, pair_sides[:, : 2 * hidden_width])
        down = contract_rows(dy_block, pair_sides[:, 2 * hidden_width :])
        return jnp.concatenate([gate_up, down], axis=1).astype(jnp.bfloat16)

    total = terms(chip).astype(jnp.float32)
    y_index, x_index = chip // X_HI, chip % X_HI
    for dy, dx in ((2, 1), (2, 0), (1, 1), (3, 1), (1, 0), (3, 0), (0, 1)):
        target = (y_index + dy) % Y * X_HI + (x_index ^ dx)
        total = total + chip_shift(terms(target), dy, dx).astype(jnp.float32)

    grads = total.astype(jnp.bfloat16)
    grad_wg = grads[None, :, :hidden_width]
    grad_wu = grads[None, :, hidden_width : 2 * hidden_width]
    grad_wd = grads[None, :, 2 * hidden_width :]
    outputs = contract_rows(selector, back_y).astype(jnp.bfloat16)
    input_grad = contract_rows(selector, back_dx).astype(jnp.bfloat16)
    return (outputs, input_grad, grad_wg, grad_wu, grad_wd)


def solution(mesh):
    in_specs = (
        P(("ep", "fsdp"), None),
        P(("ep", "fsdp"), None),
        P(("ep", "fsdp"), None),
        P("ep", "fsdp", None),
        P("ep", "fsdp", None),
        P("ep", "fsdp", None),
    )
    out_specs = (
        P(("ep", "fsdp"), None),
        P(("ep", "fsdp"), None),
        P("ep", "fsdp", None),
        P("ep", "fsdp", None),
        P("ep", "fsdp", None),
    )
    return jax.shard_map(local, mesh=mesh, in_specs=in_specs, out_specs=out_specs, check_vma=False)
```

```python
import jax
import jax.numpy as jnp
from jax import lax
from jax.sharding import PartitionSpec as P


def slot_matrix(bucket, expert_count, capacity):
    token_count = bucket.shape[0]
    labels = lax.broadcasted_iota(jnp.int32, (token_count, expert_count), 1)
    chosen = (bucket == labels).astype(jnp.int32)
    earlier = jnp.cumsum(chosen, axis=0) - chosen
    slot_index = jnp.sum(earlier * chosen, axis=1)
    position = bucket[:, 0] * capacity + slot_index
    targets = lax.broadcasted_iota(jnp.int32, (expert_count * capacity, token_count), 0)
    return (targets == position[None, :]).astype(jnp.bfloat16)


def contract_rows(left_rows, right_rows):
    return lax.dot_general(
        left_rows, right_rows, (((0,), (0,)), ((), ())), preferred_element_type=jnp.float32
    )


def contract_cols(left_rows, right_rows):
    return lax.dot_general(
        left_rows, right_rows, (((1,), (1,)), ((), ())), preferred_element_type=jnp.float32
    )


def exchange(rows, expert_count):
    row_count, width = rows.shape
    chunk = row_count // expert_count * (width // 128)
    sent = rows.reshape(row_count, width // 128, 128).reshape(expert_count, chunk, 128)
    arrived = lax.all_to_all(sent, "ep", split_axis=0, concat_axis=0, tiled=True)
    return arrived.reshape(row_count, width // 128, 128).reshape(row_count, width)


Y, X_HI = 4, 2
SHIFTS = ((2, 1), (2, 0), (1, 1), (3, 1), (1, 0), (3, 0), (0, 1))


def core_swap(array):
    return lax.ppermute(array, "fsdp", [(f, f ^ 1) for f in range(2 * Y * X_HI)])


def chip_shift(array, dy, dx):
    pairs = []
    for y in range(Y):
        for x in range(X_HI):
            for core in range(2):
                pairs.append(
                    ((y * X_HI + x) * 2 + core, ((y + dy) % Y * X_HI + (x ^ dx)) * 2 + core)
                )
    return lax.ppermute(array, "fsdp", pairs)


def chip_at(chip, dy, dx):
    return lax.bitwise_and(chip // X_HI + dy, Y - 1) * X_HI + lax.bitwise_xor(chip % X_HI, dx)


def gather_weights(shard, chip, core):
    rows = shard.shape[0]
    gathered = jnp.zeros((2 * Y * X_HI * rows, shard.shape[1]), shard.dtype)
    parts = [(chip, shard)]
    for dy, dx in SHIFTS:
        parts.append((chip_at(chip, Y - dy, dx), chip_shift(shard, dy, dx)))
    for origin, part in parts:
        gathered = lax.dynamic_update_slice(gathered, part, ((origin * 2 + core) * rows, 0))
    for group in (parts[:4], parts[4:]):
        swapped = core_swap(jnp.concatenate([part for _, part in group], axis=0))
        for number, (origin, _) in enumerate(group):
            gathered = lax.dynamic_update_slice(
                gathered,
                swapped[number * rows : (number + 1) * rows],
                ((origin * 2 + 1 - core) * rows, 0),
            )
    return gathered


def local(tokens, cotangent, bucket, w_gate, w_up, w_down):
    token_count = tokens.shape[0]
    model_width = tokens.shape[1]
    expert_count = lax.axis_size("ep")
    capacity = max(2, 5 * token_count // (4 * expert_count))
    shard_width = w_gate.shape[1]
    hidden_width = w_gate.shape[2]
    place = lax.axis_index("fsdp")
    core = lax.bitwise_and(place, 1)
    chip = lax.shift_right_logical(place, 1)

    selector = slot_matrix(bucket, expert_count, capacity)
    joined = jnp.concatenate([tokens, cotangent], axis=1)
    packed = jnp.dot(selector, joined, preferred_element_type=jnp.float32).astype(jnp.bfloat16)
    arrived = exchange(packed, expert_count)
    rows_x = arrived[:, :model_width]
    rows_dy = arrived[:, model_width:]

    weights = gather_weights(
        jnp.concatenate([w_gate[0], w_up[0], w_down[0]], axis=1), chip, core
    )
    w_gate_up = weights[:, : 2 * hidden_width]
    w_out = weights[:, 2 * hidden_width :]
    pre = jnp.dot(rows_x, w_gate_up, preferred_element_type=jnp.float32)
    gate_pre = pre[:, :hidden_width]
    up_proj = pre[:, hidden_width:]
    sigmoid_gate = jax.nn.sigmoid(gate_pre)
    activated = gate_pre * sigmoid_gate
    hidden = (activated * up_proj).astype(jnp.bfloat16)
    rows_y = contract_cols(hidden, w_out).astype(jnp.bfloat16)
    grad_hidden = jnp.dot(rows_dy, w_out, preferred_element_type=jnp.float32)
    grad_pre_gate = (
        grad_hidden * up_proj * sigmoid_gate * (1.0 + gate_pre * (1.0 - sigmoid_gate))
    ).astype(jnp.bfloat16)
    grad_pre_up = (grad_hidden * activated).astype(jnp.bfloat16)
    grads_pre = jnp.concatenate([grad_pre_gate, grad_pre_up], axis=1)
    rows_dx = contract_cols(grads_pre, w_gate_up).astype(jnp.bfloat16)
    returned = jnp.concatenate([rows_y, rows_dx], axis=1)
    sides = jnp.concatenate([grads_pre, hidden], axis=1)
    returned, arrived, sides = lax.optimization_barrier((returned, arrived, sides))
    back = exchange(returned, expert_count)

    other_rows = core_swap(arrived)
    other_sides = core_swap(sides)

    def terms(target):
        column = (target * 2 + core) * shard_width

        def block(start):
            return jnp.concatenate(
                [
                    lax.dynamic_slice_in_dim(rows, start, shard_width, axis=1)
                    for rows in (arrived, other_rows)
                ],
                axis=0,
            )

        both = jnp.concatenate([sides, other_sides], axis=0)
        gate_up = contract_rows(block(column), both[:, : 2 * hidden_width])
        down = contract_rows(block(model_width + column), both[:, 2 * hidden_width :])
        return jnp.concatenate([gate_up, down], axis=1).astype(jnp.bfloat16)

    total = terms(chip).astype(jnp.float32)
    for dy, dx in SHIFTS:
        total = total + chip_shift(terms(chip_at(chip, dy, dx)), dy, dx).astype(jnp.float32)

    grads = total.astype(jnp.bfloat16)
    grad_wg = grads[None, :, :hidden_width]
    grad_wu = grads[None, :, hidden_width : 2 * hidden_width]
    grad_wd = grads[None, :, 2 * hidden_width :]
    outputs = contract_rows(selector, back[:, :model_width]).astype(jnp.bfloat16)
    input_grad = contract_rows(selector, back[:, model_width:]).astype(jnp.bfloat16)
    return (outputs, input_grad, grad_wg, grad_wu, grad_wd)


def solution(mesh):
    in_specs = (
        P(("ep", "fsdp"), None),
        P(("ep", "fsdp"), None),
        P(("ep", "fsdp"), None),
        P("ep", "fsdp", None),
        P("ep", "fsdp", None),
        P("ep", "fsdp", None),
    )
    out_specs = (
        P(("ep", "fsdp"), None),
        P(("ep", "fsdp"), None),
        P("ep", "fsdp", None),
        P("ep", "fsdp", None),
        P("ep", "fsdp", None),
    )
    return jax.shard_map(local, mesh=mesh, in_specs=in_specs, out_specs=out_specs, check_vma=False)
```

```python
import jax
import jax.numpy as jnp
from jax import lax
from jax.experimental import pallas as pl
from jax.experimental.pallas import tpu as pltpu
from jax.sharding import PartitionSpec as P


def slot_matrix(bucket, expert_count, capacity):
    token_count = bucket.shape[0]
    labels = lax.broadcasted_iota(jnp.int32, (token_count, expert_count), 1)
    chosen = (bucket == labels).astype(jnp.int32)
    earlier = jnp.cumsum(chosen, axis=0) - chosen
    slot_index = jnp.sum(earlier * chosen, axis=1)
    position = bucket[:, 0] * capacity + slot_index
    targets = lax.broadcasted_iota(jnp.int32, (expert_count * capacity, token_count), 0)
    return (targets == position[None, :]).astype(jnp.bfloat16)


def contract_rows(left_rows, right_rows):
    return lax.dot_general(
        left_rows, right_rows, (((0,), (0,)), ((), ())), preferred_element_type=jnp.float32
    )


def contract_cols(left_rows, right_rows):
    return lax.dot_general(
        left_rows, right_rows, (((1,), (1,)), ((), ())), preferred_element_type=jnp.float32
    )


def exchange(rows, expert_count):
    row_count, width = rows.shape
    chunk = row_count // expert_count * (width // 128)
    sent = rows.reshape(row_count, width // 128, 128).reshape(expert_count, chunk, 128)
    arrived = lax.all_to_all(sent, "ep", split_axis=0, concat_axis=0, tiled=True)
    return arrived.reshape(row_count, width // 128, 128).reshape(row_count, width)


Y, X_HI = 4, 2
SHIFTS = ((2, 1), (2, 0), (1, 1), (3, 1), (1, 0), (3, 0), (0, 1))


def core_swap(array):
    return lax.ppermute(array, "fsdp", [(f, f ^ 1) for f in range(2 * Y * X_HI)])


def chip_shift(array, dy, dx):
    pairs = []
    for y in range(Y):
        for x in range(X_HI):
            for core in range(2):
                pairs.append(
                    ((y * X_HI + x) * 2 + core, ((y + dy) % Y * X_HI + (x ^ dx)) * 2 + core)
                )
    return lax.ppermute(array, "fsdp", pairs)


def chip_at(chip, dy, dx):
    return lax.bitwise_and(chip // X_HI + dy, Y - 1) * X_HI + lax.bitwise_xor(chip % X_HI, dx)


def gather_weights(shard, chip, core):
    origins = [chip] + [chip_at(chip, Y - dy, dx) for dy, dx in SHIFTS]
    parts = [shard] + [chip_shift(shard, dy, dx) for dy, dx in SHIFTS]
    groups, numbers = [], []
    for first in (4, 0):
        held = jnp.concatenate(parts[first : first + 4], axis=0)
        for array, side in ((held, core), (core_swap(held), 1 - core)):
            groups.append(array)
            numbers += [origin * 2 + side for origin in origins[first : first + 4]]
    return groups, jnp.stack(numbers).astype(jnp.int32)


def expert_kernel(numbers, rows, *refs):
    groups, (back, sides, pre, grad_hidden) = refs[:4], refs[4:]
    block = groups[0].shape[0] // 4
    width = rows.shape[1] // 2
    hidden_width = sides.shape[1] // 3

    def columns(number):
        return pl.ds(pl.multiple_of(numbers[number] * block, block), block)

    def dy_columns(number):
        return pl.ds(pl.multiple_of(width + numbers[number] * block, block), block)

    for group in range(4):
        for half in range(2):
            first = group * 4 + half * 2
            weights = groups[group].at[pl.ds(half * 2 * block, 2 * block)]
            x = jnp.concatenate([rows[:, columns(first)], rows[:, columns(first + 1)]], axis=1)
            dy = jnp.concatenate(
                [rows[:, dy_columns(first)], rows[:, dy_columns(first + 1)]], axis=1
            )
            x_part = jnp.dot(
                x, weights[:, : 2 * hidden_width], preferred_element_type=jnp.float32
            )
            dy_part = jnp.dot(
                dy, weights[:, 2 * hidden_width :], preferred_element_type=jnp.float32
            )
            if first == 0:
                pre[...] = x_part
                grad_hidden[...] = dy_part
            else:
                pre[...] += x_part
                grad_hidden[...] += dy_part

    gate_pre = pre[:, :hidden_width]
    up_proj = pre[:, hidden_width:]
    upstream = grad_hidden[...]
    sigmoid_gate = jax.nn.sigmoid(gate_pre)
    activated = gate_pre * sigmoid_gate
    sides[:, :hidden_width] = (
        upstream * up_proj * sigmoid_gate * (1.0 + gate_pre * (1.0 - sigmoid_gate))
    ).astype(sides.dtype)
    sides[:, hidden_width : 2 * hidden_width] = (upstream * activated).astype(sides.dtype)
    sides[:, 2 * hidden_width :] = (activated * up_proj).astype(sides.dtype)

    hidden = sides[:, 2 * hidden_width :]
    grads_pre = sides[:, : 2 * hidden_width]
    for group in range(4):
        for half in range(2):
            first = group * 4 + half * 2
            weights = groups[group].at[pl.ds(half * 2 * block, 2 * block)]
            y = contract_cols(hidden, weights[:, 2 * hidden_width :]).astype(back.dtype)
            dx = contract_cols(grads_pre, weights[:, : 2 * hidden_width]).astype(back.dtype)
            for number in range(2):
                part = slice(number * block, (number + 1) * block)
                back[:, columns(first + number)] = y[:, part]
                back[:, dy_columns(first + number)] = dx[:, part]


def expert_rows(rows, groups, numbers, hidden_width):
    row_count, width = rows.shape
    vmem = pl.BlockSpec(memory_space=pltpu.VMEM)
    return pl.pallas_call(
        expert_kernel,
        out_shape=(
            jax.ShapeDtypeStruct((row_count, width), rows.dtype),
            jax.ShapeDtypeStruct((row_count, 3 * hidden_width), rows.dtype),
        ),
        in_specs=[pl.BlockSpec(memory_space=pltpu.SMEM)] + [vmem] * 5,
        out_specs=(vmem, vmem),
        scratch_shapes=[
            pltpu.VMEM((row_count, 2 * hidden_width), jnp.float32),
            pltpu.VMEM((row_count, hidden_width), jnp.float32),
        ],
        compiler_params=pltpu.CompilerParams(vmem_limit_bytes=32 * 1024 * 1024),
    )(numbers, rows, *groups)


def terms_kernel(numbers, own, other, own_sides, other_sides, *terms):
    block = terms[0].shape[0]
    width = own.shape[1] // 2
    hidden_width = own_sides.shape[1] // 3
    for number, term in enumerate(terms):
        start = numbers[number] * block

        def rows(first):
            columns = pl.ds(pl.multiple_of(first + start, block), block)
            return own[:, columns], other[:, columns]

        for first, sides in ((0, slice(0, 2 * hidden_width)), (width, slice(2 * hidden_width, None))):
            own_rows, other_rows = rows(first)
            total = contract_rows(own_rows, own_sides[:, sides])
            total += contract_rows(other_rows, other_sides[:, sides])
            term[:, sides] = total.astype(term.dtype)


def gradient_terms(numbers, own, other, own_sides, other_sides, block):
    vmem = pl.BlockSpec(memory_space=pltpu.VMEM)
    count = numbers.shape[0]
    return pl.pallas_call(
        terms_kernel,
        out_shape=[jax.ShapeDtypeStruct((block, own_sides.shape[1]), own.dtype)] * count,
        in_specs=[pl.BlockSpec(memory_space=pltpu.SMEM)] + [vmem] * 4,
        out_specs=[vmem] * count,
        compiler_params=pltpu.CompilerParams(vmem_limit_bytes=32 * 1024 * 1024),
    )(numbers, own, other, own_sides, other_sides)


def local(tokens, cotangent, bucket, w_gate, w_up, w_down):
    token_count = tokens.shape[0]
    model_width = tokens.shape[1]
    expert_count = lax.axis_size("ep")
    capacity = max(2, 5 * token_count // (4 * expert_count))
    shard_width = w_gate.shape[1]
    hidden_width = w_gate.shape[2]
    place = lax.axis_index("fsdp")
    core = lax.bitwise_and(place, 1)
    chip = lax.shift_right_logical(place, 1)

    selector = slot_matrix(bucket, expert_count, capacity)
    joined = jnp.concatenate([tokens, cotangent], axis=1)
    packed = jnp.dot(selector, joined, preferred_element_type=jnp.float32).astype(jnp.bfloat16)
    shard = jnp.concatenate([w_gate[0], w_up[0], w_down[0]], axis=1)
    packed, shard = lax.optimization_barrier((packed, shard))
    arrived = exchange(packed, expert_count)
    groups, numbers = gather_weights(shard, chip, core)
    returned, sides = expert_rows(arrived, groups, numbers, hidden_width)
    returned, arrived, sides = lax.optimization_barrier((returned, arrived, sides))
    back = exchange(returned, expert_count)

    other_rows = core_swap(arrived)
    other_sides = core_swap(sides)

    targets = [chip] + [chip_at(chip, dy, dx) for dy, dx in SHIFTS]
    columns = jnp.stack([target * 2 + core for target in targets]).astype(jnp.int32)
    terms = gradient_terms(columns, arrived, other_rows, sides, other_sides, shard_width)
    total = terms[0].astype(jnp.float32)
    for (dy, dx), term in zip(SHIFTS, terms[1:]):
        total = total + chip_shift(term, dy, dx).astype(jnp.float32)

    grads = total.astype(jnp.bfloat16)
    grad_wg = grads[None, :, :hidden_width]
    grad_wu = grads[None, :, hidden_width : 2 * hidden_width]
    grad_wd = grads[None, :, 2 * hidden_width :]
    outputs = contract_rows(selector, back[:, :model_width]).astype(jnp.bfloat16)
    input_grad = contract_rows(selector, back[:, model_width:]).astype(jnp.bfloat16)
    return (outputs, input_grad, grad_wg, grad_wu, grad_wd)


def solution(mesh):
    in_specs = (
        P(("ep", "fsdp"), None),
        P(("ep", "fsdp"), None),
        P(("ep", "fsdp"), None),
        P("ep", "fsdp", None),
        P("ep", "fsdp", None),
        P("ep", "fsdp", None),
    )
    out_specs = (
        P(("ep", "fsdp"), None),
        P(("ep", "fsdp"), None),
        P("ep", "fsdp", None),
        P("ep", "fsdp", None),
        P("ep", "fsdp", None),
    )
    return jax.shard_map(local, mesh=mesh, in_specs=in_specs, out_specs=out_specs, check_vma=False)
```

```python
import functools
import jax
import jax.numpy as jnp
from jax import lax
from jax.experimental import pallas as pl
from jax.experimental.pallas import tpu as pltpu
from jax.sharding import PartitionSpec as P


def contract_rows(left_rows, right_rows):
    return lax.dot_general(
        left_rows, right_rows, (((0,), (0,)), ((), ())), preferred_element_type=jnp.float32
    )


def contract_cols(left_rows, right_rows):
    return lax.dot_general(
        left_rows, right_rows, (((1,), (1,)), ((), ())), preferred_element_type=jnp.float32
    )


def slot_matrix(bucket, expert_count, capacity):
    token_count = bucket.shape[1]
    labels = lax.broadcasted_iota(jnp.int32, (expert_count, token_count), 0)
    chosen = jnp.where(bucket == labels, 1.0, 0.0)
    before = lax.broadcasted_iota(jnp.int32, (token_count, token_count), 0)
    after = lax.broadcasted_iota(jnp.int32, (token_count, token_count), 1)
    earlier = jnp.dot(
        chosen.astype(jnp.bfloat16),
        jnp.where(before < after, 1.0, 0.0).astype(jnp.bfloat16),
        preferred_element_type=jnp.float32,
    )
    slot = jnp.sum(earlier * chosen, axis=0, keepdims=True).astype(jnp.int32)
    position = bucket * capacity + slot
    targets = lax.broadcasted_iota(jnp.int32, (expert_count * capacity, token_count), 0)
    return jnp.where(targets == position, 1.0, 0.0).astype(jnp.bfloat16)


def vmem_call(kernel, out_shape, small, *arrays, scratch_shapes=()):
    vmem = pl.BlockSpec(memory_space=pltpu.VMEM)
    in_specs = [vmem] * len(arrays)
    if small is not None:
        in_specs = [pl.BlockSpec(memory_space=pltpu.SMEM)] + in_specs
        arrays = (small, *arrays)
    return pl.pallas_call(
        kernel,
        out_shape=out_shape,
        in_specs=in_specs,
        out_specs=jax.tree.map(lambda _: vmem, out_shape),
        scratch_shapes=scratch_shapes,
        compiler_params=pltpu.CompilerParams(vmem_limit_bytes=20 * 1024 * 1024),
    )(*arrays)


def pack_kernel(expert_count, capacity, bucket, tokens, cotangent, packed):
    selector = slot_matrix(bucket[...], expert_count, capacity)
    lanes = packed.shape[2]
    columns = []
    for array in (tokens, cotangent):
        rows = jnp.dot(selector, array[...], preferred_element_type=jnp.float32)
        rows = rows.astype(packed.dtype)
        columns += [rows[:, i : i + lanes] for i in range(0, rows.shape[1], lanes)]
    packed[...] = jnp.swapaxes(jnp.stack(columns, axis=0), 0, 1)


def unpack_kernel(expert_count, capacity, bucket, back, outputs, input_grad):
    selector = slot_matrix(bucket[...], expert_count, capacity)
    lanes = back.shape[2]
    blocks = jnp.swapaxes(back[...], 0, 1)
    count = blocks.shape[0] // 2
    for first, result in ((0, outputs), (count, input_grad)):
        for pair in range(0, count, 2):
            rows = jnp.concatenate([blocks[first + pair], blocks[first + pair + 1]], axis=1)
            result[:, pair * lanes : (pair + 2) * lanes] = contract_rows(selector, rows).astype(
                result.dtype
            )


def exchange(rows, expert_count):
    row_count, blocks, lanes = rows.shape
    sent = rows.reshape(expert_count, row_count // expert_count * blocks, lanes)
    arrived = lax.all_to_all(sent, "ep", split_axis=0, concat_axis=0, tiled=True)
    return arrived.reshape(rows.shape)


Y, X_HI = 4, 2
SHIFTS = ((2, 1), (2, 0), (1, 1), (3, 1), (1, 0), (3, 0), (0, 1))


def core_swap(array):
    return lax.ppermute(array, "fsdp", [(f, f ^ 1) for f in range(2 * Y * X_HI)])


def chip_shift(array, dy, dx):
    pairs = []
    for y in range(Y):
        for x in range(X_HI):
            for core in range(2):
                pairs.append(
                    ((y * X_HI + x) * 2 + core, ((y + dy) % Y * X_HI + (x ^ dx)) * 2 + core)
                )
    return lax.ppermute(array, "fsdp", pairs)


def chip_at(chip, dy, dx):
    return lax.bitwise_and(chip // X_HI + dy, Y - 1) * X_HI + lax.bitwise_xor(chip % X_HI, dx)


def gather_weights(shard, chip, core):
    origins = [chip] + [chip_at(chip, Y - dy, dx) for dy, dx in SHIFTS]
    parts = [shard] + [chip_shift(shard, dy, dx) for dy, dx in SHIFTS]
    groups, numbers = [], []
    for first in (4, 0):
        held = jnp.concatenate(parts[first : first + 4], axis=0)
        for array, side in ((held, core), (core_swap(held), 1 - core)):
            groups.append(array)
            numbers += [origin * 2 + side for origin in origins[first : first + 4]]
    return groups, jnp.stack(numbers).astype(jnp.int32)


def expert_kernel(numbers, arrived, *refs):
    groups, (back, sides, rows, results, pre, grad_hidden) = refs[:4], refs[4:]
    block = arrived.shape[2]
    blocks = arrived.shape[1] // 2
    hidden_width = sides.shape[1] // 3
    rows[...] = jnp.swapaxes(arrived[...], 0, 1)

    for first in range(0, 16, 2):
        weights = groups[first // 4].at[pl.ds(first % 4 * block, 2 * block)]
        one, two = numbers[first], numbers[first + 1]
        x = jnp.concatenate([rows[one], rows[two]], axis=1)
        dy = jnp.concatenate([rows[blocks + one], rows[blocks + two]], axis=1)
        x_part = jnp.dot(x, weights[:, : 2 * hidden_width], preferred_element_type=jnp.float32)
        dy_part = jnp.dot(dy, weights[:, 2 * hidden_width :], preferred_element_type=jnp.float32)
        if first == 0:
            pre[...] = x_part
            grad_hidden[...] = dy_part
        else:
            pre[...] += x_part
            grad_hidden[...] += dy_part

    gate_pre = pre[:, :hidden_width]
    up_proj = pre[:, hidden_width:]
    upstream = grad_hidden[...]
    sigmoid_gate = jax.nn.sigmoid(gate_pre)
    activated = gate_pre * sigmoid_gate
    sides[:, :hidden_width] = (
        upstream * up_proj * sigmoid_gate * (1.0 + gate_pre * (1.0 - sigmoid_gate))
    ).astype(sides.dtype)
    sides[:, hidden_width : 2 * hidden_width] = (upstream * activated).astype(sides.dtype)
    sides[:, 2 * hidden_width :] = (activated * up_proj).astype(sides.dtype)

    hidden = sides[:, 2 * hidden_width :]
    grads_pre = sides[:, : 2 * hidden_width]
    for first in range(0, 16, 2):
        weights = groups[first // 4].at[pl.ds(first % 4 * block, 2 * block)]
        y = contract_cols(hidden, weights[:, 2 * hidden_width :]).astype(back.dtype)
        dx = contract_cols(grads_pre, weights[:, : 2 * hidden_width]).astype(back.dtype)
        for half in range(2):
            number = numbers[first + half]
            results[number] = y[:, half * block : (half + 1) * block]
            results[blocks + number] = dx[:, half * block : (half + 1) * block]
    back[...] = jnp.swapaxes(results[...], 0, 1)


def expert_rows(arrived, groups, numbers, hidden_width):
    row_count, blocks, lanes = arrived.shape
    return vmem_call(
        expert_kernel,
        (
            jax.ShapeDtypeStruct(arrived.shape, arrived.dtype),
            jax.ShapeDtypeStruct((row_count, 3 * hidden_width), arrived.dtype),
            jax.ShapeDtypeStruct((blocks, row_count, lanes), arrived.dtype),
        ),
        numbers,
        arrived,
        *groups,
        scratch_shapes=[
            pltpu.VMEM((blocks, row_count, lanes), arrived.dtype),
            pltpu.VMEM((row_count, 2 * hidden_width), jnp.float32),
            pltpu.VMEM((row_count, hidden_width), jnp.float32),
        ],
    )


def terms_kernel(numbers, own, other, own_sides, other_sides, *terms):
    blocks = own.shape[0] // 2
    hidden_width = own_sides.shape[1] // 3
    for place, term in enumerate(terms):
        number = numbers[place]
        for first, sides in ((0, slice(0, 2 * hidden_width)), (blocks, slice(2 * hidden_width, None))):
            total = contract_rows(own[first + number], own_sides[:, sides])
            total += contract_rows(other[first + number], other_sides[:, sides])
            term[:, sides] = total.astype(term.dtype)


def local(tokens, cotangent, bucket, w_gate, w_up, w_down):
    token_count, model_width = tokens.shape
    expert_count = lax.axis_size("ep")
    capacity = max(2, 5 * token_count // (4 * expert_count))
    slot_rows = expert_count * capacity
    shard_width = w_gate.shape[1]
    hidden_width = w_gate.shape[2]
    place = lax.axis_index("fsdp")
    core = lax.bitwise_and(place, 1)
    chip = lax.shift_right_logical(place, 1)
    sizes = (expert_count, capacity)
    choice = bucket.reshape(1, token_count)

    blocked = jax.ShapeDtypeStruct(
        (slot_rows, 2 * model_width // shard_width, shard_width), tokens.dtype
    )
    packed = vmem_call(
        functools.partial(pack_kernel, *sizes), blocked, None, choice, tokens, cotangent
    )
    packed, w_gate, w_up, w_down = lax.optimization_barrier((packed, w_gate, w_up, w_down))
    arrived = exchange(packed, expert_count)
    shard = jnp.concatenate([w_gate[0], w_up[0], w_down[0]], axis=1)
    groups, numbers = gather_weights(shard, chip, core)
    returned, sides, rows = expert_rows(arrived, groups, numbers, hidden_width)
    returned, rows, sides = lax.optimization_barrier((returned, rows, sides))
    back = exchange(returned, expert_count)

    other_rows = core_swap(rows)
    other_sides = core_swap(sides)
    targets = [chip] + [chip_at(chip, dy, dx) for dy, dx in SHIFTS]
    columns = jnp.stack([target * 2 + core for target in targets]).astype(jnp.int32)
    term = jax.ShapeDtypeStruct((shard_width, 3 * hidden_width), tokens.dtype)
    terms = vmem_call(
        terms_kernel, [term] * len(targets), columns, rows, other_rows, sides, other_sides
    )
    total = terms[0].astype(jnp.float32)
    for (dy, dx), term in zip(SHIFTS, terms[1:]):
        total = total + chip_shift(term, dy, dx).astype(jnp.float32)

    grads = total.astype(jnp.bfloat16)
    grad_wg = grads[None, :, :hidden_width]
    grad_wu = grads[None, :, hidden_width : 2 * hidden_width]
    grad_wd = grads[None, :, 2 * hidden_width :]
    result = jax.ShapeDtypeStruct(tokens.shape, tokens.dtype)
    outputs, input_grad = vmem_call(
        functools.partial(unpack_kernel, *sizes), (result, result), None, choice, back
    )
    return (outputs, input_grad, grad_wg, grad_wu, grad_wd)


def solution(mesh):
    in_specs = (
        P(("ep", "fsdp"), None),
        P(("ep", "fsdp"), None),
        P(("ep", "fsdp"), None),
        P("ep", "fsdp", None),
        P("ep", "fsdp", None),
        P("ep", "fsdp", None),
    )
    out_specs = (
        P(("ep", "fsdp"), None),
        P(("ep", "fsdp"), None),
        P("ep", "fsdp", None),
        P("ep", "fsdp", None),
        P("ep", "fsdp", None),
    )
    return jax.shard_map(local, mesh=mesh, in_specs=in_specs, out_specs=out_specs, check_vma=False)
```

```python
import functools
import jax
import jax.numpy as jnp
from jax import lax
from jax.experimental import pallas as pl
from jax.experimental.pallas import tpu as pltpu
from jax.sharding import PartitionSpec as P


def contract_rows(left_rows, right_rows):
    return lax.dot_general(
        left_rows, right_rows, (((0,), (0,)), ((), ())), preferred_element_type=jnp.float32
    )


def contract_cols(left_rows, right_rows):
    return lax.dot_general(
        left_rows, right_rows, (((1,), (1,)), ((), ())), preferred_element_type=jnp.float32
    )


def slot_matrix(bucket, expert_count, capacity):
    token_count = bucket.shape[1]
    labels = lax.broadcasted_iota(jnp.int32, (expert_count, token_count), 0)
    chosen = jnp.where(bucket == labels, 1.0, 0.0)
    before = lax.broadcasted_iota(jnp.int32, (token_count, token_count), 0)
    after = lax.broadcasted_iota(jnp.int32, (token_count, token_count), 1)
    earlier = jnp.dot(
        chosen.astype(jnp.bfloat16),
        jnp.where(before < after, 1.0, 0.0).astype(jnp.bfloat16),
        preferred_element_type=jnp.float32,
    )
    slot = jnp.sum(earlier * chosen, axis=0, keepdims=True).astype(jnp.int32)
    position = bucket * capacity + slot
    targets = lax.broadcasted_iota(jnp.int32, (expert_count * capacity, token_count), 0)
    return jnp.where(targets == position, 1.0, 0.0).astype(jnp.bfloat16)


def vmem_call(kernel, out_shape, small, *arrays, scratch_shapes=(), far_out=False):
    vmem, far = pl.BlockSpec(memory_space=pltpu.VMEM), pl.BlockSpec(memory_space=pltpu.HBM)
    in_specs = [vmem] * len(arrays)
    if small is not None:
        in_specs = [pl.BlockSpec(memory_space=pltpu.SMEM)] + in_specs
        arrays = (small, *arrays)
    return pl.pallas_call(
        kernel,
        out_shape=jax.tree.map(lambda s: pltpu.HBM(s.shape, s.dtype), out_shape) if far_out else out_shape,
        in_specs=in_specs,
        out_specs=jax.tree.map(lambda _: far if far_out else vmem, out_shape),
        scratch_shapes=scratch_shapes,
        compiler_params=pltpu.CompilerParams(vmem_limit_bytes=20 * 1024 * 1024),
    )(*arrays)


def pack_kernel(
    expert_count, capacity, bucket, tokens, cotangent, packed, choice, near, result, sems
):
    lookup = pltpu.make_async_copy(bucket, choice, sems.at[4])
    lookup.start()
    loads = [
        pltpu.make_async_copy(array, near.at[number], sems.at[number])
        for number, array in enumerate((tokens, cotangent))
    ]
    for load in loads:
        load.start()
    lookup.wait()
    selector = slot_matrix(choice[...], expert_count, capacity)
    lanes = packed.shape[2]
    count = packed.shape[1] // 2
    stores = []
    for number, load in enumerate(loads):
        load.wait()
        rows = jnp.dot(selector, near[number], preferred_element_type=jnp.float32)
        rows = rows.astype(packed.dtype)
        columns = [rows[:, i : i + lanes] for i in range(0, rows.shape[1], lanes)]
        part = pl.ds(number * count, count)
        result[:, part, :] = jnp.swapaxes(jnp.stack(columns, axis=0), 0, 1)
        stores.append(
            pltpu.make_async_copy(result.at[:, part], packed.at[:, part], sems.at[2 + number])
        )
        stores[-1].start()
    for store in stores:
        store.wait()


def pack_rows(kernel, out_shape, choice, tokens, cotangent):
    far = pl.BlockSpec(memory_space=pltpu.HBM)
    return pl.pallas_call(
        kernel,
        out_shape=pltpu.HBM(out_shape.shape, out_shape.dtype),
        in_specs=[far, far, far],
        out_specs=far,
        scratch_shapes=[
            pltpu.VMEM(choice.shape, choice.dtype),
            pltpu.VMEM((2, *tokens.shape), tokens.dtype),
            pltpu.VMEM(out_shape.shape, out_shape.dtype),
            pltpu.SemaphoreType.DMA((5,)),
        ],
        compiler_params=pltpu.CompilerParams(vmem_limit_bytes=20 * 1024 * 1024),
    )(*(pltpu.with_memory_space_constraint(a, pltpu.HBM) for a in (choice, tokens, cotangent)))


def unpack_kernel(expert_count, capacity, bucket, back, outputs, input_grad):
    selector = slot_matrix(bucket[...], expert_count, capacity)
    lanes = back.shape[2]
    blocks = jnp.swapaxes(back[...], 0, 1)
    count = blocks.shape[0] // 2
    for first, result in ((0, outputs), (count, input_grad)):
        for pair in range(0, count, 2):
            rows = jnp.concatenate([blocks[first + pair], blocks[first + pair + 1]], axis=1)
            result[:, pair * lanes : (pair + 2) * lanes] = contract_rows(selector, rows).astype(
                result.dtype
            )


def exchange(rows, expert_count):
    row_count, blocks, lanes = rows.shape
    sent = rows.reshape(expert_count, row_count // expert_count * blocks, lanes)
    arrived = lax.all_to_all(sent, "ep", split_axis=0, concat_axis=0, tiled=True)
    return arrived.reshape(rows.shape)


Y, X_HI = 4, 2


def core_swap(array):
    return lax.ppermute(array, "fsdp", [(f, f ^ 1) for f in range(2 * Y * X_HI)])


def chip_shift(array, dy, dx):
    pairs = []
    for y in range(Y):
        for x in range(X_HI):
            for core in range(2):
                pairs.append(
                    ((y * X_HI + x) * 2 + core, ((y + dy) % Y * X_HI + (x ^ dx)) * 2 + core)
                )
    return lax.ppermute(array, "fsdp", pairs)


def chip_at(chip, dy, dx):
    return lax.bitwise_and(chip // X_HI + dy, Y - 1) * X_HI + lax.bitwise_xor(chip % X_HI, dx)


def gather_weights(shard, chip, core):
    across, two = chip_shift(shard, 0, 1), chip_shift(shard, 2, 0)
    one, three = chip_shift(shard, 1, 0), chip_shift(shard, 3, 0)
    early = [(shard, 0, 0), (across, 0, 1), (one, 3, 0), (three, 1, 0)]
    late = [
        (two, 2, 0),
        (chip_shift(across, 1, 0), 3, 1),
        (chip_shift(across, 3, 0), 1, 1),
        (chip_shift(two, 0, 1), 2, 1),
    ]
    groups, numbers = [], []
    for parts in (early, late):
        held = jnp.concatenate([part for part, _, _ in parts], axis=0)
        for array, side in ((held, core), (core_swap(held), 1 - core)):
            groups.append(array)
            numbers += [chip_at(chip, dy, dx) * 2 + side for _, dy, dx in parts]
    return groups, jnp.stack(numbers).astype(jnp.int32)


def expert_kernel(numbers, arrived, *refs):
    groups, (back, sides_out, rows_out) = refs[:4], refs[4:7]
    rows, results, returned, sides, pre, grad_hidden, sems = refs[7:]
    block = arrived.shape[2]
    blocks = arrived.shape[1] // 2
    hidden_width = sides.shape[1] // 3
    rows[...] = jnp.swapaxes(arrived[...], 0, 1)
    stores = [pltpu.make_async_copy(rows, rows_out, sems.at[0])]
    stores[0].start()

    for first in range(0, 16, 2):
        weights = groups[first // 4].at[pl.ds(first % 4 * block, 2 * block)]
        one, two = numbers[first], numbers[first + 1]
        x = jnp.concatenate([rows[one], rows[two]], axis=1)
        dy = jnp.concatenate([rows[blocks + one], rows[blocks + two]], axis=1)
        x_part = jnp.dot(x, weights[:, : 2 * hidden_width], preferred_element_type=jnp.float32)
        dy_part = jnp.dot(dy, weights[:, 2 * hidden_width :], preferred_element_type=jnp.float32)
        if first == 0:
            pre[...] = x_part
            grad_hidden[...] = dy_part
        else:
            pre[...] += x_part
            grad_hidden[...] += dy_part

    gate_pre = pre[:, :hidden_width]
    up_proj = pre[:, hidden_width:]
    upstream = grad_hidden[...]
    sigmoid_gate = jax.nn.sigmoid(gate_pre)
    activated = gate_pre * sigmoid_gate
    sides[:, :hidden_width] = (
        upstream * up_proj * sigmoid_gate * (1.0 + gate_pre * (1.0 - sigmoid_gate))
    ).astype(sides.dtype)
    sides[:, hidden_width : 2 * hidden_width] = (upstream * activated).astype(sides.dtype)
    sides[:, 2 * hidden_width :] = (activated * up_proj).astype(sides.dtype)
    stores.append(pltpu.make_async_copy(sides, sides_out, sems.at[1]))
    stores[1].start()

    hidden = sides[:, 2 * hidden_width :]
    grads_pre = sides[:, : 2 * hidden_width]
    for first in range(0, 16, 2):
        weights = groups[first // 4].at[pl.ds(first % 4 * block, 2 * block)]
        y = contract_cols(hidden, weights[:, 2 * hidden_width :]).astype(back.dtype)
        dx = contract_cols(grads_pre, weights[:, : 2 * hidden_width]).astype(back.dtype)
        for half in range(2):
            number = numbers[first + half]
            results[number] = y[:, half * block : (half + 1) * block]
            results[blocks + number] = dx[:, half * block : (half + 1) * block]
    step = back.shape[0] // 5
    for number in range(5):
        part = pl.ds(number * step, step)
        returned[part] = jnp.swapaxes(results[:, part], 0, 1)
        stores.append(
            pltpu.make_async_copy(returned.at[part], back.at[part], sems.at[2 + number])
        )
        stores[-1].start()
    for store in stores:
        store.wait()


def expert_rows(arrived, groups, numbers, hidden_width):
    row_count, blocks, lanes = arrived.shape
    return vmem_call(
        expert_kernel,
        (
            jax.ShapeDtypeStruct(arrived.shape, arrived.dtype),
            jax.ShapeDtypeStruct((row_count, 3 * hidden_width), arrived.dtype),
            jax.ShapeDtypeStruct((blocks, row_count, lanes), arrived.dtype),
        ),
        numbers,
        arrived,
        *groups,
        scratch_shapes=[
            pltpu.VMEM((blocks, row_count, lanes), arrived.dtype),
            pltpu.VMEM((blocks, row_count, lanes), arrived.dtype),
            pltpu.VMEM(arrived.shape, arrived.dtype),
            pltpu.VMEM((row_count, 3 * hidden_width), arrived.dtype),
            pltpu.VMEM((row_count, 2 * hidden_width), jnp.float32),
            pltpu.VMEM((row_count, hidden_width), jnp.float32),
            pltpu.SemaphoreType.DMA((7,)),
        ],
        far_out=True,
    )


def terms_kernel(numbers, own, other, own_sides, other_sides, *terms):
    blocks = own.shape[0] // 2
    hidden_width = own_sides.shape[1] // 3
    for place, term in enumerate(terms):
        number = numbers[place]
        for first, sides in ((0, slice(0, 2 * hidden_width)), (blocks, slice(2 * hidden_width, None))):
            total = contract_rows(own[first + number], own_sides[:, sides])
            total += contract_rows(other[first + number], other_sides[:, sides])
            term[:, sides] = total.astype(term.dtype)


def local(tokens, cotangent, bucket, w_gate, w_up, w_down):
    token_count, model_width = tokens.shape
    expert_count = lax.axis_size("ep")
    capacity = max(2, 5 * token_count // (4 * expert_count))
    slot_rows = expert_count * capacity
    shard_width = w_gate.shape[1]
    hidden_width = w_gate.shape[2]
    place = lax.axis_index("fsdp")
    core = lax.bitwise_and(place, 1)
    chip = lax.shift_right_logical(place, 1)
    sizes = (expert_count, capacity)
    choice = bucket.reshape(1, token_count)

    blocked = jax.ShapeDtypeStruct(
        (slot_rows, 2 * model_width // shard_width, shard_width), tokens.dtype
    )
    packed = pack_rows(functools.partial(pack_kernel, *sizes), blocked, choice, tokens, cotangent)
    packed, w_gate, w_up, w_down = lax.optimization_barrier((packed, w_gate, w_up, w_down))
    arrived = exchange(packed, expert_count)
    shard = jnp.concatenate([w_gate[0], w_up[0], w_down[0]], axis=1)
    groups, numbers = gather_weights(shard, chip, core)
    returned, sides, rows = expert_rows(arrived, groups, numbers, hidden_width)
    returned, rows, sides = lax.optimization_barrier((returned, rows, sides))
    back = exchange(returned, expert_count)

    other_rows = core_swap(rows)
    other_sides = core_swap(sides)
    targets = [(dy, dx) for dy in range(Y) for dx in range(X_HI)]
    columns = jnp.stack([chip_at(chip, dy, dx) * 2 + core for dy, dx in targets]).astype(jnp.int32)
    shape = jax.ShapeDtypeStruct((shard_width, 3 * hidden_width), tokens.dtype)
    terms = vmem_call(
        terms_kernel, [shape] * len(targets), columns, rows, other_rows, sides, other_sides
    )
    terms = dict(zip(targets, terms))

    def add(*arrays):
        return sum(array.astype(jnp.float32) for array in arrays)

    def summed(*arrays):
        return add(*arrays).astype(tokens.dtype)

    two = summed(terms[2, 0], chip_shift(terms[2, 1], 0, 1))
    across = summed(
        terms[0, 1], chip_shift(terms[1, 1], 1, 0), chip_shift(terms[3, 1], 3, 0)
    )
    total = add(
        terms[0, 0],
        chip_shift(terms[1, 0], 1, 0),
        chip_shift(terms[3, 0], 3, 0),
        chip_shift(two, 2, 0),
        chip_shift(across, 0, 1),
    )

    grads = total.astype(jnp.bfloat16)
    grad_wg = grads[None, :, :hidden_width]
    grad_wu = grads[None, :, hidden_width : 2 * hidden_width]
    grad_wd = grads[None, :, 2 * hidden_width :]
    result = jax.ShapeDtypeStruct(tokens.shape, tokens.dtype)
    outputs, input_grad = vmem_call(
        functools.partial(unpack_kernel, *sizes), (result, result), None, choice, back
    )
    return (outputs, input_grad, grad_wg, grad_wu, grad_wd)


def solution(mesh):
    in_specs = (
        P(("ep", "fsdp"), None),
        P(("ep", "fsdp"), None),
        P(("ep", "fsdp"), None),
        P("ep", "fsdp", None),
        P("ep", "fsdp", None),
        P("ep", "fsdp", None),
    )
    out_specs = (
        P(("ep", "fsdp"), None),
        P(("ep", "fsdp"), None),
        P("ep", "fsdp", None),
        P("ep", "fsdp", None),
        P("ep", "fsdp", None),
    )
    return jax.shard_map(local, mesh=mesh, in_specs=in_specs, out_specs=out_specs, check_vma=False)
```

```python
import functools
import jax
import jax.numpy as jnp
from jax import lax
from jax.experimental import pallas as pl
from jax.experimental.pallas import tpu as pltpu
from jax.sharding import PartitionSpec as P


def contract_rows(left_rows, right_rows):
    return lax.dot_general(
        left_rows, right_rows, (((0,), (0,)), ((), ())), preferred_element_type=jnp.float32
    )


def contract_cols(left_rows, right_rows):
    return lax.dot_general(
        left_rows, right_rows, (((1,), (1,)), ((), ())), preferred_element_type=jnp.float32
    )


def slot_matrix(bucket, expert_count, capacity):
    token_count = bucket.shape[1]
    labels = lax.broadcasted_iota(jnp.int32, (expert_count, token_count), 0)
    chosen = jnp.where(bucket == labels, 1.0, 0.0)
    before = lax.broadcasted_iota(jnp.int32, (token_count, token_count), 0)
    after = lax.broadcasted_iota(jnp.int32, (token_count, token_count), 1)
    earlier = jnp.dot(
        chosen.astype(jnp.bfloat16),
        jnp.where(before < after, 1.0, 0.0).astype(jnp.bfloat16),
        preferred_element_type=jnp.float32,
    )
    slot = jnp.sum(earlier * chosen, axis=0, keepdims=True).astype(jnp.int32)
    position = bucket * capacity + slot
    targets = lax.broadcasted_iota(jnp.int32, (expert_count * capacity, token_count), 0)
    return jnp.where(targets == position, 1.0, 0.0).astype(jnp.bfloat16)


def vmem_call(kernel, out_shape, small, *arrays, scratch_shapes=(), far_out=False):
    vmem, far = pl.BlockSpec(memory_space=pltpu.VMEM), pl.BlockSpec(memory_space=pltpu.HBM)
    in_specs = [vmem] * len(arrays)
    if small is not None:
        in_specs = [pl.BlockSpec(memory_space=pltpu.SMEM)] + in_specs
        arrays = (small, *arrays)
    return pl.pallas_call(
        kernel,
        out_shape=jax.tree.map(lambda s: pltpu.HBM(s.shape, s.dtype), out_shape) if far_out else out_shape,
        in_specs=in_specs,
        out_specs=jax.tree.map(lambda _: far if far_out else vmem, out_shape),
        scratch_shapes=scratch_shapes,
        compiler_params=pltpu.CompilerParams(vmem_limit_bytes=20 * 1024 * 1024),
    )(*arrays)


def pack_kernel(
    expert_count, capacity, bucket, tokens, cotangent, packed, choice, near, result, sems
):
    lookup = pltpu.make_async_copy(bucket, choice, sems.at[4])
    lookup.start()
    loads = [
        pltpu.make_async_copy(array, near.at[number], sems.at[number])
        for number, array in enumerate((tokens, cotangent))
    ]
    for load in loads:
        load.start()
    lookup.wait()
    selector = slot_matrix(choice[...], expert_count, capacity)
    lanes = packed.shape[2]
    count = packed.shape[1] // 2
    stores = []
    for number, load in enumerate(loads):
        load.wait()
        rows = jnp.dot(selector, near[number], preferred_element_type=jnp.float32)
        rows = rows.astype(packed.dtype)
        columns = [rows[:, i : i + lanes] for i in range(0, rows.shape[1], lanes)]
        part = pl.ds(number * count, count)
        result[:, part, :] = jnp.swapaxes(jnp.stack(columns, axis=0), 0, 1)
        stores.append(
            pltpu.make_async_copy(result.at[:, part], packed.at[:, part], sems.at[2 + number])
        )
        stores[-1].start()
    for store in stores:
        store.wait()


def pack_rows(kernel, out_shape, choice, tokens, cotangent):
    far = pl.BlockSpec(memory_space=pltpu.HBM)
    return pl.pallas_call(
        kernel,
        out_shape=pltpu.HBM(out_shape.shape, out_shape.dtype),
        in_specs=[far, far, far],
        out_specs=far,
        scratch_shapes=[
            pltpu.VMEM(choice.shape, choice.dtype),
            pltpu.VMEM((2, *tokens.shape), tokens.dtype),
            pltpu.VMEM(out_shape.shape, out_shape.dtype),
            pltpu.SemaphoreType.DMA((5,)),
        ],
        compiler_params=pltpu.CompilerParams(vmem_limit_bytes=20 * 1024 * 1024),
    )(*(pltpu.with_memory_space_constraint(a, pltpu.HBM) for a in (choice, tokens, cotangent)))


def unpack_kernel(expert_count, capacity, bucket, back, outputs, input_grad):
    selector = slot_matrix(bucket[...], expert_count, capacity)
    lanes = back.shape[2]
    blocks = jnp.swapaxes(back[...], 0, 1)
    count = blocks.shape[0] // 2
    for first, result in ((0, outputs), (count, input_grad)):
        for pair in range(0, count, 2):
            rows = jnp.concatenate([blocks[first + pair], blocks[first + pair + 1]], axis=1)
            result[:, pair * lanes : (pair + 2) * lanes] = contract_rows(selector, rows).astype(
                result.dtype
            )


def exchange(rows, expert_count):
    row_count, blocks, lanes = rows.shape
    sent = rows.reshape(expert_count, row_count // expert_count * blocks, lanes)
    arrived = lax.all_to_all(sent, "ep", split_axis=0, concat_axis=0, tiled=True)
    return arrived.reshape(rows.shape)


Y, X_HI = 4, 2


def core_swap(array):
    return lax.ppermute(array, "fsdp", [(f, f ^ 1) for f in range(2 * Y * X_HI)])


def chip_shift(array, dy, dx):
    pairs = []
    for y in range(Y):
        for x in range(X_HI):
            for core in range(2):
                pairs.append(
                    ((y * X_HI + x) * 2 + core, ((y + dy) % Y * X_HI + (x ^ dx)) * 2 + core)
                )
    return lax.ppermute(array, "fsdp", pairs)


def chip_at(chip, dy, dx):
    return lax.bitwise_and(chip // X_HI + dy, Y - 1) * X_HI + lax.bitwise_xor(chip % X_HI, dx)


def gather_weights(shard, chip, core):
    across, two = chip_shift(shard, 0, 1), chip_shift(shard, 2, 0)
    one, three = chip_shift(shard, 1, 0), chip_shift(shard, 3, 0)
    early = [(shard, 0, 0), (one, 3, 0), (three, 1, 0), (chip_shift(across, 1, 0), 3, 1)]
    late = [(across, 0, 1), (two, 2, 0), (chip_shift(across, 3, 0), 1, 1), (chip_shift(two, 0, 1), 2, 1)]
    groups, numbers = [], []
    for parts in (early, late):
        held = jnp.concatenate([part for part, _, _ in parts], axis=0)
        for array, side in ((held, core), (core_swap(held), 1 - core)):
            groups.append(array)
            numbers += [chip_at(chip, dy, dx) * 2 + side for _, dy, dx in parts]
    return groups, jnp.stack(numbers).astype(jnp.int32)


def expert_kernel(numbers, arrived, *refs):
    groups, (back, sides_out, rows_out) = refs[:4], refs[4:7]
    x_rows, dy_rows, y_blocks, dx_blocks, y_back, dx_back, sides, pre, grad_hidden, sems = refs[7:]
    block = arrived.shape[2]
    blocks = arrived.shape[1] // 2
    hidden_width = sides.shape[1] // 3
    stores = []

    def store(source, target):
        stores.append(pltpu.make_async_copy(source, target, sems.at[len(stores)]))
        stores[-1].start()

    pairs = [
        group.at[pl.ds(start, 2 * block)]
        for group in groups
        for start in range(0, group.shape[0], 2 * block)
    ]

    def product(rows, columns, total):
        for place, weights in enumerate(pairs):
            both = [rows[numbers[2 * place + half]] for half in range(2)]
            part = jnp.dot(
                jnp.concatenate(both, axis=1),
                weights[:, columns],
                preferred_element_type=jnp.float32,
            )
            if place == 0:
                total[...] = part
            else:
                total[...] += part

    def back_product(left, columns, result):
        for place, weights in enumerate(pairs):
            part = contract_cols(left, weights[:, columns]).astype(result.dtype)
            for half in range(2):
                result[numbers[2 * place + half]] = part[:, half * block : (half + 1) * block]

    gate_up, down = slice(0, 2 * hidden_width), slice(2 * hidden_width, 3 * hidden_width)
    x_rows[...] = jnp.swapaxes(arrived[:, :blocks], 0, 1)
    store(x_rows, rows_out.at[pl.ds(0, blocks)])
    dy_rows[...] = jnp.swapaxes(arrived[:, blocks:], 0, 1)
    store(dy_rows, rows_out.at[pl.ds(blocks, blocks)])

    product(x_rows, gate_up, pre)
    product(dy_rows, down, grad_hidden)
    gate_pre = pre[:, :hidden_width]
    up_proj = pre[:, hidden_width:]
    upstream = grad_hidden[...]
    sigmoid_gate = jax.nn.sigmoid(gate_pre)
    activated = gate_pre * sigmoid_gate
    hidden = (activated * up_proj).astype(sides.dtype)
    sides[:, down] = hidden
    sides[:, :hidden_width] = (
        upstream * up_proj * sigmoid_gate * (1.0 + gate_pre * (1.0 - sigmoid_gate))
    ).astype(sides.dtype)
    sides[:, hidden_width : 2 * hidden_width] = (upstream * activated).astype(sides.dtype)
    store(sides, sides_out)

    back_product(hidden, down, y_blocks)
    y_back[...] = jnp.swapaxes(y_blocks[...], 0, 1)
    store(y_back, back.at[:, pl.ds(0, blocks)])
    back_product(sides[:, gate_up], gate_up, dx_blocks)
    step = back.shape[0] // 5
    for number in range(5):
        part = pl.ds(number * step, step)
        dx_back[part] = jnp.swapaxes(dx_blocks[:, part], 0, 1)
        store(dx_back.at[part], back.at[part, pl.ds(blocks, blocks)])
    for copy in stores:
        copy.wait()


def expert_rows(arrived, groups, numbers, hidden_width):
    row_count, blocks, lanes = arrived.shape
    return vmem_call(
        expert_kernel,
        (
            jax.ShapeDtypeStruct(arrived.shape, arrived.dtype),
            jax.ShapeDtypeStruct((row_count, 3 * hidden_width), arrived.dtype),
            jax.ShapeDtypeStruct((blocks, row_count, lanes), arrived.dtype),
        ),
        numbers,
        arrived,
        *groups,
        scratch_shapes=[
            *[pltpu.VMEM((blocks // 2, row_count, lanes), arrived.dtype)] * 4,
            *[pltpu.VMEM((row_count, blocks // 2, lanes), arrived.dtype)] * 2,
            pltpu.VMEM((row_count, 3 * hidden_width), arrived.dtype),
            pltpu.VMEM((row_count, 2 * hidden_width), jnp.float32),
            pltpu.VMEM((row_count, hidden_width), jnp.float32),
            pltpu.SemaphoreType.DMA((9,)),
        ],
        far_out=True,
    )


def terms_kernel(numbers, own, other, own_sides, other_sides, *terms):
    blocks = own.shape[0] // 2
    hidden_width = own_sides.shape[1] // 3
    for place, term in enumerate(terms):
        number = numbers[place]
        for first, sides in ((0, slice(0, 2 * hidden_width)), (blocks, slice(2 * hidden_width, None))):
            total = contract_rows(own[first + number], own_sides[:, sides])
            total += contract_rows(other[first + number], other_sides[:, sides])
            term[:, sides] = total.astype(term.dtype)


def local(tokens, cotangent, bucket, w_gate, w_up, w_down):
    token_count, model_width = tokens.shape
    expert_count = lax.axis_size("ep")
    capacity = max(2, 5 * token_count // (4 * expert_count))
    slot_rows = expert_count * capacity
    shard_width = w_gate.shape[1]
    hidden_width = w_gate.shape[2]
    place = lax.axis_index("fsdp")
    core = lax.bitwise_and(place, 1)
    chip = lax.shift_right_logical(place, 1)
    sizes = (expert_count, capacity)
    choice = bucket.reshape(1, token_count)

    blocked = jax.ShapeDtypeStruct(
        (slot_rows, 2 * model_width // shard_width, shard_width), tokens.dtype
    )
    packed = pack_rows(functools.partial(pack_kernel, *sizes), blocked, choice, tokens, cotangent)
    packed, w_gate, w_up, w_down = lax.optimization_barrier((packed, w_gate, w_up, w_down))
    arrived = exchange(packed, expert_count)
    shard = jnp.concatenate([w_gate[0], w_up[0], w_down[0]], axis=1)
    groups, numbers = gather_weights(shard, chip, core)
    returned, sides, rows = expert_rows(arrived, groups, numbers, hidden_width)
    returned, rows, sides = lax.optimization_barrier((returned, rows, sides))
    back = exchange(returned, expert_count)

    other_rows = core_swap(rows)
    other_sides = core_swap(sides)
    targets = [(dy, dx) for dy in range(Y) for dx in range(X_HI)]
    columns = jnp.stack([chip_at(chip, dy, dx) * 2 + core for dy, dx in targets]).astype(jnp.int32)
    shape = jax.ShapeDtypeStruct((shard_width, 3 * hidden_width), tokens.dtype)
    terms = vmem_call(
        terms_kernel, [shape] * len(targets), columns, rows, other_rows, sides, other_sides
    )
    terms = dict(zip(targets, terms))

    def add(*arrays):
        return sum(array.astype(jnp.float32) for array in arrays)

    def summed(*arrays):
        return add(*arrays).astype(tokens.dtype)

    two = summed(terms[2, 0], chip_shift(terms[2, 1], 0, 1))
    across = summed(
        terms[0, 1], chip_shift(terms[1, 1], 1, 0), chip_shift(terms[3, 1], 3, 0)
    )
    total = add(
        terms[0, 0],
        chip_shift(terms[1, 0], 1, 0),
        chip_shift(terms[3, 0], 3, 0),
        chip_shift(two, 2, 0),
        chip_shift(across, 0, 1),
    )

    grads = total.astype(jnp.bfloat16)
    grad_wg = grads[None, :, :hidden_width]
    grad_wu = grads[None, :, hidden_width : 2 * hidden_width]
    grad_wd = grads[None, :, 2 * hidden_width :]
    result = jax.ShapeDtypeStruct(tokens.shape, tokens.dtype)
    outputs, input_grad = vmem_call(
        functools.partial(unpack_kernel, *sizes), (result, result), None, choice, back
    )
    return (outputs, input_grad, grad_wg, grad_wu, grad_wd)


def solution(mesh):
    in_specs = (
        P(("ep", "fsdp"), None),
        P(("ep", "fsdp"), None),
        P(("ep", "fsdp"), None),
        P("ep", "fsdp", None),
        P("ep", "fsdp", None),
        P("ep", "fsdp", None),
    )
    out_specs = (
        P(("ep", "fsdp"), None),
        P(("ep", "fsdp"), None),
        P("ep", "fsdp", None),
        P("ep", "fsdp", None),
        P("ep", "fsdp", None),
    )
    return jax.shard_map(local, mesh=mesh, in_specs=in_specs, out_specs=out_specs, check_vma=False)
```

```python
import functools
import jax
import jax.numpy as jnp
from jax import lax
from jax.experimental import pallas as pl
from jax.experimental.pallas import tpu as pltpu
from jax.sharding import PartitionSpec as P


def contract_rows(left_rows, right_rows):
    return lax.dot_general(
        left_rows, right_rows, (((0,), (0,)), ((), ())), preferred_element_type=jnp.float32
    )


STRIDE = 5


def slot_matrix(bucket, expert_count, capacity):
    token_count = bucket.shape[1]
    labels = lax.broadcasted_iota(jnp.int32, (expert_count, token_count), 0)
    chosen = jnp.where(bucket == labels, 1.0, 0.0)
    before = lax.broadcasted_iota(jnp.int32, (token_count, token_count), 0)
    after = lax.broadcasted_iota(jnp.int32, (token_count, token_count), 1)
    earlier = jnp.dot(
        chosen.astype(jnp.bfloat16),
        jnp.where(before < after, 1.0, 0.0).astype(jnp.bfloat16),
        preferred_element_type=jnp.float32,
    )
    slot = jnp.sum(earlier * chosen, axis=0, keepdims=True).astype(jnp.int32)
    place = lax.rem(bucket * pow(STRIDE, -1, expert_count), expert_count)
    position = place * capacity + slot
    targets = lax.broadcasted_iota(jnp.int32, (expert_count * capacity, token_count), 0)
    return jnp.where(targets == position, 1.0, 0.0).astype(jnp.bfloat16)


def vmem_call(kernel, out_shape, small, *arrays, scratch_shapes=(), far_out=False):
    vmem, far = pl.BlockSpec(memory_space=pltpu.VMEM), pl.BlockSpec(memory_space=pltpu.HBM)
    in_specs = [vmem] * len(arrays)
    if small is not None:
        in_specs = [pl.BlockSpec(memory_space=pltpu.SMEM)] + in_specs
        arrays = (small, *arrays)
    return pl.pallas_call(
        kernel,
        out_shape=jax.tree.map(lambda s: pltpu.HBM(s.shape, s.dtype), out_shape) if far_out else out_shape,
        in_specs=in_specs,
        out_specs=jax.tree.map(lambda _: far if far_out else vmem, out_shape),
        scratch_shapes=scratch_shapes,
        compiler_params=pltpu.CompilerParams(vmem_limit_bytes=20 * 1024 * 1024),
    )(*arrays)


def pack_kernel(
    expert_count,
    capacity,
    bucket,
    tokens,
    cotangent,
    packed,
    selector_out,
    choice,
    near,
    result,
    selector,
    sems,
):
    lookup = pltpu.make_async_copy(bucket, choice, sems.at[4])
    lookup.start()
    loads = [
        pltpu.make_async_copy(array, near.at[number], sems.at[number])
        for number, array in enumerate((tokens, cotangent))
    ]
    for load in loads:
        load.start()
    lookup.wait()
    selector[...] = slot_matrix(choice[...], expert_count, capacity)
    stores = [pltpu.make_async_copy(selector, selector_out, sems.at[5])]
    stores[0].start()
    lanes = packed.shape[2]
    count = packed.shape[1] // 2
    for number, load in enumerate(loads):
        load.wait()
        rows = jnp.dot(selector[...], near[number], preferred_element_type=jnp.float32)
        rows = rows.astype(packed.dtype)
        columns = [rows[:, i : i + lanes] for i in range(0, rows.shape[1], lanes)]
        part = pl.ds(number * count, count)
        result[:, part, :] = jnp.swapaxes(jnp.stack(columns, axis=0), 0, 1)
        stores.append(
            pltpu.make_async_copy(result.at[:, part], packed.at[:, part], sems.at[2 + number])
        )
        stores[-1].start()
    for store in stores:
        store.wait()


def pack_rows(kernel, out_shape, choice, tokens, cotangent):
    selector = jax.ShapeDtypeStruct((out_shape.shape[0], tokens.shape[0]), tokens.dtype)
    far = pl.BlockSpec(memory_space=pltpu.HBM)
    return pl.pallas_call(
        kernel,
        out_shape=tuple(pltpu.HBM(shape.shape, shape.dtype) for shape in (out_shape, selector)),
        in_specs=[far, far, far],
        out_specs=(far, far),
        scratch_shapes=[
            pltpu.VMEM(choice.shape, choice.dtype),
            pltpu.VMEM((2, *tokens.shape), tokens.dtype),
            pltpu.VMEM(out_shape.shape, out_shape.dtype),
            pltpu.VMEM(selector.shape, selector.dtype),
            pltpu.SemaphoreType.DMA((6,)),
        ],
        compiler_params=pltpu.CompilerParams(vmem_limit_bytes=20 * 1024 * 1024),
    )(*(pltpu.with_memory_space_constraint(a, pltpu.HBM) for a in (choice, tokens, cotangent)))


def unpack_kernel(selector, back, outputs, input_grad, results, sems):
    lanes = back.shape[2]
    count = back.shape[1] // 2
    stores = []
    for number, target in enumerate((outputs, input_grad)):
        blocks = jnp.swapaxes(back[:, number * count : (number + 1) * count], 0, 1)
        for pair in range(0, count, 2):
            rows = jnp.concatenate([blocks[pair], blocks[pair + 1]], axis=1)
            results[number, :, pair * lanes : (pair + 2) * lanes] = contract_rows(
                selector[...], rows
            ).astype(results.dtype)
        stores.append(pltpu.make_async_copy(results.at[number], target, sems.at[number]))
        stores[-1].start()
    for store in stores:
        store.wait()


def exchange(rows, expert_count):
    row_count, blocks, lanes = rows.shape
    sent = rows.reshape(expert_count, row_count // expert_count * blocks, lanes)
    order = [number * STRIDE % expert_count for number in range(expert_count)]
    arrived = lax.all_to_all(
        sent, "ep", split_axis=0, concat_axis=0, tiled=True, axis_index_groups=[order]
    )
    return arrived.reshape(rows.shape)


Y, X_HI = 4, 2


def core_swap(array):
    return lax.ppermute(array, "fsdp", [(f, f ^ 1) for f in range(2 * Y * X_HI)])


def chip_shift(array, dy, dx):
    pairs = []
    for y in range(Y):
        for x in range(X_HI):
            for core in range(2):
                pairs.append(
                    ((y * X_HI + x) * 2 + core, ((y + dy) % Y * X_HI + (x ^ dx)) * 2 + core)
                )
    return lax.ppermute(array, "fsdp", pairs)


def chip_at(chip, dy, dx):
    return lax.bitwise_and(chip // X_HI + dy, Y - 1) * X_HI + lax.bitwise_xor(chip % X_HI, dx)


def gather_weights(shard, chip, core):
    across, two = chip_shift(shard, 0, 1), chip_shift(shard, 2, 0)
    one, three = chip_shift(shard, 1, 0), chip_shift(shard, 3, 0)
    early = [(shard, 0, 0), (one, 3, 0), (three, 1, 0), (chip_shift(across, 1, 0), 3, 1)]
    late = [(across, 0, 1), (two, 2, 0), (chip_shift(across, 3, 0), 1, 1), (chip_shift(two, 0, 1), 2, 1)]
    groups, numbers = [], []
    for parts in (early, late):
        held = jnp.concatenate([part for part, _, _ in parts], axis=0)
        for array, side in ((held, core), (core_swap(held), 1 - core)):
            groups.append(array)
            numbers += [chip_at(chip, dy, dx) * 2 + side for _, dy, dx in parts]
    return groups, jnp.stack(numbers).astype(jnp.int32)


def expert_kernel(numbers, arrived, *refs):
    groups, (back, sides_out, rows_out) = refs[:4], refs[4:7]
    x_rows, dy_rows, y_blocks, dx_blocks, y_back, dx_back, sides, pre, grad_hidden, sems = refs[7:]
    block = arrived.shape[2]
    blocks = arrived.shape[1] // 2
    hidden_width = sides.shape[1] // 3
    stores = []

    def store(source, target):
        stores.append(pltpu.make_async_copy(source, target, sems.at[len(stores)]))
        stores[-1].start()

    pairs = [
        group.at[pl.ds(start, 2 * block)]
        for group in groups
        for start in range(0, group.shape[0], 2 * block)
    ]

    def product(rows, columns, total):
        for place, weights in enumerate(pairs):
            both = [rows[numbers[2 * place + half]] for half in range(2)]
            part = jnp.dot(
                jnp.concatenate(both, axis=1),
                weights[:, columns],
                preferred_element_type=jnp.float32,
            )
            if place == 0:
                total[...] = part
            else:
                total[...] += part

    def back_product(left, columns, result):
        left = left.T
        for place, weights in enumerate(pairs):
            part = jnp.dot(weights[:, columns], left, preferred_element_type=jnp.float32)
            part = part.T.astype(result.dtype)
            for half in range(2):
                result[numbers[2 * place + half]] = part[:, half * block : (half + 1) * block]

    gate_up, down = slice(0, 2 * hidden_width), slice(2 * hidden_width, 3 * hidden_width)
    x_rows[...] = jnp.swapaxes(arrived[:, :blocks], 0, 1)
    store(x_rows, rows_out.at[pl.ds(0, blocks)])
    dy_rows[...] = jnp.swapaxes(arrived[:, blocks:], 0, 1)
    store(dy_rows, rows_out.at[pl.ds(blocks, blocks)])

    product(x_rows, gate_up, pre)
    product(dy_rows, down, grad_hidden)
    gate_pre = pre[:, :hidden_width]
    up_proj = pre[:, hidden_width:]
    upstream = grad_hidden[...]
    sigmoid_gate = jax.nn.sigmoid(gate_pre)
    activated = gate_pre * sigmoid_gate
    hidden = (activated * up_proj).astype(sides.dtype)
    sides[:, down] = hidden
    sides[:, :hidden_width] = (
        upstream * up_proj * sigmoid_gate * (1.0 + gate_pre * (1.0 - sigmoid_gate))
    ).astype(sides.dtype)
    sides[:, hidden_width : 2 * hidden_width] = (upstream * activated).astype(sides.dtype)
    store(sides, sides_out)

    back_product(hidden, down, y_blocks)
    y_back[...] = jnp.swapaxes(y_blocks[...], 0, 1)
    store(y_back, back.at[:, pl.ds(0, blocks)])
    back_product(sides[:, gate_up], gate_up, dx_blocks)
    step = back.shape[0] // 5
    for number in range(5):
        part = pl.ds(number * step, step)
        dx_back[part] = jnp.swapaxes(dx_blocks[:, part], 0, 1)
        store(dx_back.at[part], back.at[part, pl.ds(blocks, blocks)])
    for copy in stores:
        copy.wait()


def expert_rows(arrived, groups, numbers, hidden_width):
    row_count, blocks, lanes = arrived.shape
    return vmem_call(
        expert_kernel,
        (
            jax.ShapeDtypeStruct(arrived.shape, arrived.dtype),
            jax.ShapeDtypeStruct((row_count, 3 * hidden_width), arrived.dtype),
            jax.ShapeDtypeStruct((blocks, row_count, lanes), arrived.dtype),
        ),
        numbers,
        arrived,
        *groups,
        scratch_shapes=[
            *[pltpu.VMEM((blocks // 2, row_count, lanes), arrived.dtype)] * 4,
            *[pltpu.VMEM((row_count, blocks // 2, lanes), arrived.dtype)] * 2,
            pltpu.VMEM((row_count, 3 * hidden_width), arrived.dtype),
            pltpu.VMEM((row_count, 2 * hidden_width), jnp.float32),
            pltpu.VMEM((row_count, hidden_width), jnp.float32),
            pltpu.SemaphoreType.DMA((9,)),
        ],
        far_out=True,
    )


def terms_kernel(numbers, own, other, own_sides, other_sides, *terms):
    blocks = own.shape[0] // 2
    hidden_width = own_sides.shape[1] // 3
    for place, term in enumerate(terms):
        number = numbers[place]
        for first, sides in ((0, slice(0, 2 * hidden_width)), (blocks, slice(2 * hidden_width, None))):
            total = contract_rows(own[first + number], own_sides[:, sides])
            total += contract_rows(other[first + number], other_sides[:, sides])
            term[:, sides] = total.astype(term.dtype)


def local(tokens, cotangent, bucket, w_gate, w_up, w_down):
    token_count, model_width = tokens.shape
    expert_count = lax.axis_size("ep")
    capacity = max(2, 5 * token_count // (4 * expert_count))
    slot_rows = expert_count * capacity
    shard_width = w_gate.shape[1]
    hidden_width = w_gate.shape[2]
    place = lax.axis_index("fsdp")
    core = lax.bitwise_and(place, 1)
    chip = lax.shift_right_logical(place, 1)
    sizes = (expert_count, capacity)
    choice = bucket.reshape(1, token_count)

    blocked = jax.ShapeDtypeStruct(
        (slot_rows, 2 * model_width // shard_width, shard_width), tokens.dtype
    )
    packed, selector = pack_rows(functools.partial(pack_kernel, *sizes), blocked, choice, tokens, cotangent)
    packed, w_gate, w_up, w_down = lax.optimization_barrier((packed, w_gate, w_up, w_down))
    arrived = exchange(packed, expert_count)
    shard = jnp.concatenate([w_gate[0], w_up[0], w_down[0]], axis=1)
    groups, numbers = gather_weights(shard, chip, core)
    returned, sides, rows = expert_rows(arrived, groups, numbers, hidden_width)
    returned, rows, sides = lax.optimization_barrier((returned, rows, sides))
    back = exchange(returned, expert_count)

    other_rows = core_swap(rows)
    other_sides = core_swap(sides)
    targets = [(dy, dx) for dy in range(Y) for dx in range(X_HI)]
    columns = jnp.stack([chip_at(chip, dy, dx) * 2 + core for dy, dx in targets]).astype(jnp.int32)
    shape = jax.ShapeDtypeStruct((shard_width, 3 * hidden_width), tokens.dtype)
    terms = vmem_call(
        terms_kernel, [shape] * len(targets), columns, rows, other_rows, sides, other_sides
    )
    terms = dict(zip(targets, terms))

    def add(*arrays):
        return sum(array.astype(jnp.float32) for array in arrays)

    def summed(*arrays):
        return add(*arrays).astype(tokens.dtype)

    two = summed(terms[2, 0], chip_shift(terms[2, 1], 0, 1))
    across = summed(
        terms[0, 1], chip_shift(terms[1, 1], 1, 0), chip_shift(terms[3, 1], 3, 0)
    )
    total = add(
        terms[0, 0],
        chip_shift(terms[1, 0], 1, 0),
        chip_shift(terms[3, 0], 3, 0),
        chip_shift(two, 2, 0),
        chip_shift(across, 0, 1),
    )

    grads = total.astype(jnp.bfloat16)
    grad_wg = grads[None, :, :hidden_width]
    grad_wu = grads[None, :, hidden_width : 2 * hidden_width]
    grad_wd = grads[None, :, 2 * hidden_width :]
    result = jax.ShapeDtypeStruct(tokens.shape, tokens.dtype)
    outputs, input_grad = vmem_call(
        unpack_kernel,
        (result, result),
        None,
        selector,
        back,
        scratch_shapes=[
            pltpu.VMEM((2, *tokens.shape), tokens.dtype),
            pltpu.SemaphoreType.DMA((2,)),
        ],
        far_out=True,
    )
    return (outputs, input_grad, grad_wg, grad_wu, grad_wd)


def solution(mesh):
    in_specs = (
        P(("ep", "fsdp"), None),
        P(("ep", "fsdp"), None),
        P(("ep", "fsdp"), None),
        P("ep", "fsdp", None),
        P("ep", "fsdp", None),
        P("ep", "fsdp", None),
    )
    out_specs = (
        P(("ep", "fsdp"), None),
        P(("ep", "fsdp"), None),
        P("ep", "fsdp", None),
        P("ep", "fsdp", None),
        P("ep", "fsdp", None),
    )
    return jax.shard_map(local, mesh=mesh, in_specs=in_specs, out_specs=out_specs, check_vma=False)
```

```python
import functools
import jax
import jax.numpy as jnp
from jax import lax
from jax.experimental import pallas as pl
from jax.experimental.pallas import tpu as pltpu
from jax.sharding import PartitionSpec as P


def contract_rows(left_rows, right_rows):
    return lax.dot_general(
        left_rows, right_rows, (((0,), (0,)), ((), ())), preferred_element_type=jnp.float32
    )


def slot_matrix(bucket, expert_count, capacity):
    token_count = bucket.shape[1]
    labels = lax.broadcasted_iota(jnp.int32, (expert_count, token_count), 0)
    chosen = jnp.where(bucket == labels, 1.0, 0.0)
    before = lax.broadcasted_iota(jnp.int32, (token_count, token_count), 0)
    after = lax.broadcasted_iota(jnp.int32, (token_count, token_count), 1)
    earlier = jnp.dot(
        chosen.astype(jnp.bfloat16),
        jnp.where(before < after, 1.0, 0.0).astype(jnp.bfloat16),
        preferred_element_type=jnp.float32,
    )
    slot = jnp.sum(earlier * chosen, axis=0, keepdims=True).astype(jnp.int32)
    position = bucket * capacity + slot
    targets = lax.broadcasted_iota(jnp.int32, (expert_count * capacity, token_count), 0)
    return jnp.where(targets == position, 1.0, 0.0).astype(jnp.bfloat16)


def vmem_call(kernel, out_shape, small, *arrays, scratch_shapes=(), far_out=False):
    vmem, far = pl.BlockSpec(memory_space=pltpu.VMEM), pl.BlockSpec(memory_space=pltpu.HBM)
    in_specs = [vmem] * len(arrays)
    if small is not None:
        in_specs = [pl.BlockSpec(memory_space=pltpu.SMEM)] + in_specs
        arrays = (small, *arrays)
    return pl.pallas_call(
        kernel,
        out_shape=jax.tree.map(lambda s: pltpu.HBM(s.shape, s.dtype), out_shape) if far_out else out_shape,
        in_specs=in_specs,
        out_specs=jax.tree.map(lambda _: far if far_out else vmem, out_shape),
        scratch_shapes=scratch_shapes,
        compiler_params=pltpu.CompilerParams(vmem_limit_bytes=20 * 1024 * 1024),
    )(*arrays)


def pack_kernel(
    expert_count,
    capacity,
    bucket,
    tokens,
    cotangent,
    packed,
    selector_out,
    choice,
    near,
    result,
    selector,
    sems,
):
    lookup = pltpu.make_async_copy(bucket, choice, sems.at[4])
    lookup.start()
    loads = [
        pltpu.make_async_copy(array, near.at[number], sems.at[number])
        for number, array in enumerate((tokens, cotangent))
    ]
    for load in loads:
        load.start()
    lookup.wait()
    selector[...] = slot_matrix(choice[...], expert_count, capacity)
    stores = [pltpu.make_async_copy(selector, selector_out, sems.at[5])]
    stores[0].start()
    lanes = packed.shape[2]
    count = packed.shape[1] // 2
    for number, load in enumerate(loads):
        load.wait()
        rows = jnp.dot(selector[...], near[number], preferred_element_type=jnp.float32)
        rows = rows.astype(packed.dtype)
        columns = [rows[:, i : i + lanes] for i in range(0, rows.shape[1], lanes)]
        part = pl.ds(number * count, count)
        result[:, part, :] = jnp.swapaxes(jnp.stack(columns, axis=0), 0, 1)
        stores.append(
            pltpu.make_async_copy(result.at[:, part], packed.at[:, part], sems.at[2 + number])
        )
        stores[-1].start()
    for store in stores:
        store.wait()


def pack_rows(kernel, out_shape, choice, tokens, cotangent):
    selector = jax.ShapeDtypeStruct((out_shape.shape[0], tokens.shape[0]), tokens.dtype)
    far = pl.BlockSpec(memory_space=pltpu.HBM)
    return pl.pallas_call(
        kernel,
        out_shape=tuple(pltpu.HBM(shape.shape, shape.dtype) for shape in (out_shape, selector)),
        in_specs=[far, far, far],
        out_specs=(far, far),
        scratch_shapes=[
            pltpu.VMEM(choice.shape, choice.dtype),
            pltpu.VMEM((2, *tokens.shape), tokens.dtype),
            pltpu.VMEM(out_shape.shape, out_shape.dtype),
            pltpu.VMEM(selector.shape, selector.dtype),
            pltpu.SemaphoreType.DMA((6,)),
        ],
        compiler_params=pltpu.CompilerParams(vmem_limit_bytes=20 * 1024 * 1024),
    )(*(pltpu.with_memory_space_constraint(a, pltpu.HBM) for a in (choice, tokens, cotangent)))


def unpack_kernel(selector, back, outputs, input_grad, results, sems):
    lanes = back.shape[2]
    count = back.shape[1] // 2
    stores = []
    for number, target in enumerate((outputs, input_grad)):
        blocks = jnp.swapaxes(back[:, number * count : (number + 1) * count], 0, 1)
        for pair in range(0, count, 2):
            rows = jnp.concatenate([blocks[pair], blocks[pair + 1]], axis=1)
            results[number, :, pair * lanes : (pair + 2) * lanes] = contract_rows(
                selector[...], rows
            ).astype(results.dtype)
        stores.append(pltpu.make_async_copy(results.at[number], target, sems.at[number]))
        stores[-1].start()
    for store in stores:
        store.wait()


def exchange(rows, expert_count):
    row_count, blocks, lanes = rows.shape
    sent = rows.reshape(expert_count, row_count // expert_count * blocks, lanes)
    arrived = lax.all_to_all(sent, "ep", split_axis=0, concat_axis=0, tiled=True)
    return arrived.reshape(rows.shape)


Y, X_HI = 4, 2


def core_swap(array):
    return lax.ppermute(array, "fsdp", [(f, f ^ 1) for f in range(2 * Y * X_HI)])


def chip_shift(array, dy, dx):
    pairs = []
    for y in range(Y):
        for x in range(X_HI):
            for core in range(2):
                pairs.append(
                    ((y * X_HI + x) * 2 + core, ((y + dy) % Y * X_HI + (x ^ dx)) * 2 + core)
                )
    return lax.ppermute(array, "fsdp", pairs)


def chip_at(chip, dy, dx):
    return lax.bitwise_and(chip // X_HI + dy, Y - 1) * X_HI + lax.bitwise_xor(chip % X_HI, dx)


def gather_weights(shard, chip, core):
    across, two = chip_shift(shard, 0, 1), chip_shift(shard, 2, 0)
    one, three = chip_shift(shard, 1, 0), chip_shift(shard, 3, 0)
    early = [(shard, 0, 0), (one, 3, 0), (three, 1, 0), (chip_shift(across, 1, 0), 3, 1)]
    late = [(across, 0, 1), (two, 2, 0), (chip_shift(across, 3, 0), 1, 1), (chip_shift(two, 0, 1), 2, 1)]
    groups, numbers = [], []
    for parts in (early, late):
        held = jnp.concatenate([part for part, _, _ in parts], axis=0)
        for array, side in ((held, core), (core_swap(held), 1 - core)):
            groups.append(array)
            numbers += [chip_at(chip, dy, dx) * 2 + side for _, dy, dx in parts]
    return groups, jnp.stack(numbers).astype(jnp.int32)


def expert_kernel(numbers, arrived, *refs):
    groups, (back, sides_out, rows_out) = refs[:4], refs[4:7]
    x_rows, dy_rows, y_blocks, dx_blocks, y_back, dx_back, sides, pre, grad_hidden, sems = refs[7:]
    block = arrived.shape[2]
    blocks = arrived.shape[1] // 2
    hidden_width = sides.shape[1] // 3
    stores = []

    def store(source, target):
        stores.append(pltpu.make_async_copy(source, target, sems.at[len(stores)]))
        stores[-1].start()

    pairs = [
        group.at[pl.ds(start, 2 * block)]
        for group in groups
        for start in range(0, group.shape[0], 2 * block)
    ]

    def product(rows, columns, total):
        for place, weights in enumerate(pairs):
            both = [rows[numbers[2 * place + half]] for half in range(2)]
            part = jnp.dot(
                jnp.concatenate(both, axis=1),
                weights[:, columns],
                preferred_element_type=jnp.float32,
            )
            if place == 0:
                total[...] = part
            else:
                total[...] += part

    def back_product(left, columns, result):
        left = left.T
        for place, weights in enumerate(pairs):
            part = jnp.dot(weights[:, columns], left, preferred_element_type=jnp.float32)
            part = part.T.astype(result.dtype)
            for half in range(2):
                result[numbers[2 * place + half]] = part[:, half * block : (half + 1) * block]

    gate_up, down = slice(0, 2 * hidden_width), slice(2 * hidden_width, 3 * hidden_width)
    x_rows[...] = jnp.swapaxes(arrived[:, :blocks], 0, 1)
    store(x_rows, rows_out.at[pl.ds(0, blocks)])
    dy_rows[...] = jnp.swapaxes(arrived[:, blocks:], 0, 1)
    store(dy_rows, rows_out.at[pl.ds(blocks, blocks)])

    product(x_rows, gate_up, pre)
    product(dy_rows, down, grad_hidden)
    gate_pre = pre[:, :hidden_width]
    up_proj = pre[:, hidden_width:]
    upstream = grad_hidden[...]
    sigmoid_gate = jax.nn.sigmoid(gate_pre)
    activated = gate_pre * sigmoid_gate
    hidden = (activated * up_proj).astype(sides.dtype)
    sides[:, down] = hidden
    sides[:, :hidden_width] = (
        upstream * up_proj * sigmoid_gate * (1.0 + gate_pre * (1.0 - sigmoid_gate))
    ).astype(sides.dtype)
    sides[:, hidden_width : 2 * hidden_width] = (upstream * activated).astype(sides.dtype)
    store(sides, sides_out)

    back_product(hidden, down, y_blocks)
    y_back[...] = jnp.swapaxes(y_blocks[...], 0, 1)
    store(y_back, back.at[:, pl.ds(0, blocks)])
    back_product(sides[:, gate_up], gate_up, dx_blocks)
    step = back.shape[0] // 5
    for number in range(5):
        part = pl.ds(number * step, step)
        dx_back[part] = jnp.swapaxes(dx_blocks[:, part], 0, 1)
        store(dx_back.at[part], back.at[part, pl.ds(blocks, blocks)])
    for copy in stores:
        copy.wait()


def expert_rows(arrived, groups, numbers, hidden_width):
    row_count, blocks, lanes = arrived.shape
    return vmem_call(
        expert_kernel,
        (
            jax.ShapeDtypeStruct(arrived.shape, arrived.dtype),
            jax.ShapeDtypeStruct((row_count, 3 * hidden_width), arrived.dtype),
            jax.ShapeDtypeStruct((blocks, row_count, lanes), arrived.dtype),
        ),
        numbers,
        arrived,
        *groups,
        scratch_shapes=[
            *[pltpu.VMEM((blocks // 2, row_count, lanes), arrived.dtype)] * 4,
            *[pltpu.VMEM((row_count, blocks // 2, lanes), arrived.dtype)] * 2,
            pltpu.VMEM((row_count, 3 * hidden_width), arrived.dtype),
            pltpu.VMEM((row_count, 2 * hidden_width), jnp.float32),
            pltpu.VMEM((row_count, hidden_width), jnp.float32),
            pltpu.SemaphoreType.DMA((9,)),
        ],
        far_out=True,
    )


def terms_kernel(numbers, own, other, own_sides, other_sides, *terms):
    blocks = own.shape[0] // 2
    hidden_width = own_sides.shape[1] // 3
    for place, term in enumerate(terms):
        number = numbers[place]
        for first, sides in ((0, slice(0, 2 * hidden_width)), (blocks, slice(2 * hidden_width, None))):
            total = contract_rows(own[first + number], own_sides[:, sides])
            total += contract_rows(other[first + number], other_sides[:, sides])
            term[:, sides] = total.astype(term.dtype)


def local(tokens, cotangent, bucket, w_gate, w_up, w_down):
    token_count, model_width = tokens.shape
    expert_count = lax.axis_size("ep")
    capacity = max(2, 5 * token_count // (4 * expert_count))
    slot_rows = expert_count * capacity
    shard_width = w_gate.shape[1]
    hidden_width = w_gate.shape[2]
    place = lax.axis_index("fsdp")
    core = lax.bitwise_and(place, 1)
    chip = lax.shift_right_logical(place, 1)
    sizes = (expert_count, capacity)
    choice = bucket.reshape(1, token_count)

    blocked = jax.ShapeDtypeStruct(
        (slot_rows, 2 * model_width // shard_width, shard_width), tokens.dtype
    )
    packed, selector = pack_rows(functools.partial(pack_kernel, *sizes), blocked, choice, tokens, cotangent)
    packed, w_gate, w_up, w_down = lax.optimization_barrier((packed, w_gate, w_up, w_down))
    arrived = exchange(packed, expert_count)
    shard = jnp.concatenate([w_gate[0], w_up[0], w_down[0]], axis=1)
    groups, numbers = gather_weights(shard, chip, core)
    returned, sides, rows = expert_rows(arrived, groups, numbers, hidden_width)
    returned, rows, sides = lax.optimization_barrier((returned, rows, sides))
    back = exchange(returned, expert_count)

    other_rows = core_swap(rows)
    other_sides = core_swap(sides)
    targets = [(dy, dx) for dy in range(Y) for dx in range(X_HI)]
    columns = jnp.stack([chip_at(chip, dy, dx) * 2 + core for dy, dx in targets]).astype(jnp.int32)
    shape = jax.ShapeDtypeStruct((shard_width, 3 * hidden_width), tokens.dtype)
    terms = vmem_call(
        terms_kernel, [shape] * len(targets), columns, rows, other_rows, sides, other_sides
    )
    terms = dict(zip(targets, terms))

    def add(*arrays):
        return sum(array.astype(jnp.float32) for array in arrays)

    def summed(*arrays):
        return add(*arrays).astype(tokens.dtype)

    two = summed(terms[2, 0], chip_shift(terms[2, 1], 0, 1))
    across = summed(
        terms[0, 1], chip_shift(terms[1, 1], 1, 0), chip_shift(terms[3, 1], 3, 0)
    )
    total = add(
        terms[0, 0],
        chip_shift(terms[1, 0], 1, 0),
        chip_shift(terms[3, 0], 3, 0),
        chip_shift(two, 2, 0),
        chip_shift(across, 0, 1),
    )

    grads = total.astype(jnp.bfloat16)
    grad_wg = grads[None, :, :hidden_width]
    grad_wu = grads[None, :, hidden_width : 2 * hidden_width]
    grad_wd = grads[None, :, 2 * hidden_width :]
    result = jax.ShapeDtypeStruct(tokens.shape, tokens.dtype)
    outputs, input_grad = vmem_call(
        unpack_kernel,
        (result, result),
        None,
        selector,
        back,
        scratch_shapes=[
            pltpu.VMEM((2, *tokens.shape), tokens.dtype),
            pltpu.SemaphoreType.DMA((2,)),
        ],
        far_out=True,
    )
    return (outputs, input_grad, grad_wg, grad_wu, grad_wd)


def solution(mesh):
    in_specs = (
        P(("ep", "fsdp"), None),
        P(("ep", "fsdp"), None),
        P(("ep", "fsdp"), None),
        P("ep", "fsdp", None),
        P("ep", "fsdp", None),
        P("ep", "fsdp", None),
    )
    out_specs = (
        P(("ep", "fsdp"), None),
        P(("ep", "fsdp"), None),
        P("ep", "fsdp", None),
        P("ep", "fsdp", None),
        P("ep", "fsdp", None),
    )
    return jax.shard_map(local, mesh=mesh, in_specs=in_specs, out_specs=out_specs, check_vma=False)
```

```python
import functools
import jax
import jax.numpy as jnp
from jax import lax
from jax.experimental import pallas as pl
from jax.experimental.pallas import tpu as pltpu
from jax.sharding import PartitionSpec as P


def contract_rows(left_rows, right_rows):
    return lax.dot_general(
        left_rows, right_rows, (((0,), (0,)), ((), ())), preferred_element_type=jnp.float32
    )


PAIR = 2


def slot_matrix(bucket, expert_count, capacity):
    token_count = bucket.shape[1]
    labels = lax.broadcasted_iota(jnp.int32, (expert_count, token_count), 0)
    chosen = jnp.where(bucket == labels, 1.0, 0.0)
    before = lax.broadcasted_iota(jnp.int32, (token_count, token_count), 0)
    after = lax.broadcasted_iota(jnp.int32, (token_count, token_count), 1)
    earlier = jnp.dot(
        chosen.astype(jnp.bfloat16),
        jnp.where(before < after, 1.0, 0.0).astype(jnp.bfloat16),
        preferred_element_type=jnp.float32,
    )
    slot = jnp.sum(earlier * chosen, axis=0, keepdims=True).astype(jnp.int32)
    within = lax.bitwise_and(bucket, PAIR - 1)
    place = expert_count - PAIR - (bucket - within) + within
    position = place * capacity + slot
    targets = lax.broadcasted_iota(jnp.int32, (expert_count * capacity, token_count), 0)
    return jnp.where(targets == position, 1.0, 0.0).astype(jnp.bfloat16)


def vmem_call(kernel, out_shape, small, *arrays, scratch_shapes=(), far_out=False):
    vmem, far = pl.BlockSpec(memory_space=pltpu.VMEM), pl.BlockSpec(memory_space=pltpu.HBM)
    in_specs = [vmem] * len(arrays)
    if small is not None:
        in_specs = [pl.BlockSpec(memory_space=pltpu.SMEM)] + in_specs
        arrays = (small, *arrays)
    return pl.pallas_call(
        kernel,
        out_shape=jax.tree.map(lambda s: pltpu.HBM(s.shape, s.dtype), out_shape) if far_out else out_shape,
        in_specs=in_specs,
        out_specs=jax.tree.map(lambda _: far if far_out else vmem, out_shape),
        scratch_shapes=scratch_shapes,
        compiler_params=pltpu.CompilerParams(vmem_limit_bytes=20 * 1024 * 1024),
    )(*arrays)


def pack_kernel(
    expert_count,
    capacity,
    bucket,
    tokens,
    cotangent,
    packed,
    selector_out,
    choice,
    near,
    result,
    selector,
    sems,
):
    lookup = pltpu.make_async_copy(bucket, choice, sems.at[4])
    lookup.start()
    loads = [
        pltpu.make_async_copy(array, near.at[number], sems.at[number])
        for number, array in enumerate((tokens, cotangent))
    ]
    for load in loads:
        load.start()
    lookup.wait()
    selector[...] = slot_matrix(choice[...], expert_count, capacity)
    stores = [pltpu.make_async_copy(selector, selector_out, sems.at[5])]
    stores[0].start()
    lanes = packed.shape[2]
    count = packed.shape[1] // 2
    for number, load in enumerate(loads):
        load.wait()
        rows = jnp.dot(selector[...], near[number], preferred_element_type=jnp.float32)
        rows = rows.astype(packed.dtype)
        columns = [rows[:, i : i + lanes] for i in range(0, rows.shape[1], lanes)]
        part = pl.ds(number * count, count)
        result[:, part, :] = jnp.swapaxes(jnp.stack(columns, axis=0), 0, 1)
        stores.append(
            pltpu.make_async_copy(result.at[:, part], packed.at[:, part], sems.at[2 + number])
        )
        stores[-1].start()
    for store in stores:
        store.wait()


def pack_rows(kernel, out_shape, choice, tokens, cotangent):
    selector = jax.ShapeDtypeStruct((out_shape.shape[0], tokens.shape[0]), tokens.dtype)
    far = pl.BlockSpec(memory_space=pltpu.HBM)
    return pl.pallas_call(
        kernel,
        out_shape=tuple(pltpu.HBM(shape.shape, shape.dtype) for shape in (out_shape, selector)),
        in_specs=[far, far, far],
        out_specs=(far, far),
        scratch_shapes=[
            pltpu.VMEM(choice.shape, choice.dtype),
            pltpu.VMEM((2, *tokens.shape), tokens.dtype),
            pltpu.VMEM(out_shape.shape, out_shape.dtype),
            pltpu.VMEM(selector.shape, selector.dtype),
            pltpu.SemaphoreType.DMA((6,)),
        ],
        compiler_params=pltpu.CompilerParams(vmem_limit_bytes=20 * 1024 * 1024),
    )(*(pltpu.with_memory_space_constraint(a, pltpu.HBM) for a in (choice, tokens, cotangent)))


def unpack_kernel(selector, back, outputs, input_grad, results, sems):
    lanes = back.shape[2]
    count = back.shape[1] // 2
    stores = []
    for number, target in enumerate((outputs, input_grad)):
        blocks = jnp.swapaxes(back[:, number * count : (number + 1) * count], 0, 1)
        for pair in range(0, count, 2):
            rows = jnp.concatenate([blocks[pair], blocks[pair + 1]], axis=1)
            results[number, :, pair * lanes : (pair + 2) * lanes] = contract_rows(
                selector[...], rows
            ).astype(results.dtype)
        stores.append(pltpu.make_async_copy(results.at[number], target, sems.at[number]))
        stores[-1].start()
    for store in stores:
        store.wait()


def exchange(rows, expert_count):
    row_count, blocks, lanes = rows.shape
    sent = rows.reshape(expert_count, row_count // expert_count * blocks, lanes)
    order = [
        first + within
        for first in reversed(range(0, expert_count, PAIR))
        for within in range(PAIR)
    ]
    arrived = lax.all_to_all(
        sent, "ep", split_axis=0, concat_axis=0, tiled=True, axis_index_groups=[order]
    )
    return arrived.reshape(rows.shape)


Y, X_HI = 4, 2


def core_swap(array):
    return lax.ppermute(array, "fsdp", [(f, f ^ 1) for f in range(2 * Y * X_HI)])


def chip_shift(array, dy, dx):
    pairs = []
    for y in range(Y):
        for x in range(X_HI):
            for core in range(2):
                pairs.append(
                    ((y * X_HI + x) * 2 + core, ((y + dy) % Y * X_HI + (x ^ dx)) * 2 + core)
                )
    return lax.ppermute(array, "fsdp", pairs)


def chip_at(chip, dy, dx):
    return lax.bitwise_and(chip // X_HI + dy, Y - 1) * X_HI + lax.bitwise_xor(chip % X_HI, dx)


def gather_weights(shard, chip, core):
    across, two = chip_shift(shard, 0, 1), chip_shift(shard, 2, 0)
    one, three = chip_shift(shard, 1, 0), chip_shift(shard, 3, 0)
    early = [(shard, 0, 0), (one, 3, 0), (three, 1, 0), (chip_shift(across, 1, 0), 3, 1)]
    late = [(across, 0, 1), (two, 2, 0), (chip_shift(across, 3, 0), 1, 1), (chip_shift(two, 0, 1), 2, 1)]
    groups, numbers = [], []
    for parts in (early, late):
        held = jnp.concatenate([part for part, _, _ in parts], axis=0)
        for array, side in ((held, core), (core_swap(held), 1 - core)):
            groups.append(array)
            numbers += [chip_at(chip, dy, dx) * 2 + side for _, dy, dx in parts]
    return groups, jnp.stack(numbers).astype(jnp.int32)


def expert_kernel(numbers, arrived, *refs):
    groups, (back, sides_out, rows_out) = refs[:4], refs[4:7]
    x_rows, dy_rows, y_blocks, dx_blocks, y_back, dx_back, sides, pre, grad_hidden, sems = refs[7:]
    block = arrived.shape[2]
    blocks = arrived.shape[1] // 2
    hidden_width = sides.shape[1] // 3
    stores = []

    def store(source, target):
        stores.append(pltpu.make_async_copy(source, target, sems.at[len(stores)]))
        stores[-1].start()

    pairs = [
        group.at[pl.ds(start, 2 * block)]
        for group in groups
        for start in range(0, group.shape[0], 2 * block)
    ]

    def product(rows, columns, total):
        for place, weights in enumerate(pairs):
            both = [rows[numbers[2 * place + half]] for half in range(2)]
            part = jnp.dot(
                jnp.concatenate(both, axis=1),
                weights[:, columns],
                preferred_element_type=jnp.float32,
            )
            if place == 0:
                total[...] = part
            else:
                total[...] += part

    def back_product(left, columns, result):
        left = left.T
        for place, weights in enumerate(pairs):
            part = jnp.dot(weights[:, columns], left, preferred_element_type=jnp.float32)
            part = part.T.astype(result.dtype)
            for half in range(2):
                result[numbers[2 * place + half]] = part[:, half * block : (half + 1) * block]

    gate_up, down = slice(0, 2 * hidden_width), slice(2 * hidden_width, 3 * hidden_width)
    x_rows[...] = jnp.swapaxes(arrived[:, :blocks], 0, 1)
    store(x_rows, rows_out.at[pl.ds(0, blocks)])
    dy_rows[...] = jnp.swapaxes(arrived[:, blocks:], 0, 1)
    store(dy_rows, rows_out.at[pl.ds(blocks, blocks)])

    product(x_rows, gate_up, pre)
    product(dy_rows, down, grad_hidden)
    gate_pre = pre[:, :hidden_width]
    up_proj = pre[:, hidden_width:]
    upstream = grad_hidden[...]
    sigmoid_gate = jax.nn.sigmoid(gate_pre)
    activated = gate_pre * sigmoid_gate
    hidden = (activated * up_proj).astype(sides.dtype)
    sides[:, down] = hidden
    sides[:, :hidden_width] = (
        upstream * up_proj * sigmoid_gate * (1.0 + gate_pre * (1.0 - sigmoid_gate))
    ).astype(sides.dtype)
    sides[:, hidden_width : 2 * hidden_width] = (upstream * activated).astype(sides.dtype)
    store(sides, sides_out)

    back_product(hidden, down, y_blocks)
    y_back[...] = jnp.swapaxes(y_blocks[...], 0, 1)
    store(y_back, back.at[:, pl.ds(0, blocks)])
    back_product(sides[:, gate_up], gate_up, dx_blocks)
    step = back.shape[0] // 5
    for number in range(5):
        part = pl.ds(number * step, step)
        dx_back[part] = jnp.swapaxes(dx_blocks[:, part], 0, 1)
        store(dx_back.at[part], back.at[part, pl.ds(blocks, blocks)])
    for copy in stores:
        copy.wait()


def expert_rows(arrived, groups, numbers, hidden_width):
    row_count, blocks, lanes = arrived.shape
    return vmem_call(
        expert_kernel,
        (
            jax.ShapeDtypeStruct(arrived.shape, arrived.dtype),
            jax.ShapeDtypeStruct((row_count, 3 * hidden_width), arrived.dtype),
            jax.ShapeDtypeStruct((blocks, row_count, lanes), arrived.dtype),
        ),
        numbers,
        arrived,
        *groups,
        scratch_shapes=[
            *[pltpu.VMEM((blocks // 2, row_count, lanes), arrived.dtype)] * 4,
            *[pltpu.VMEM((row_count, blocks // 2, lanes), arrived.dtype)] * 2,
            pltpu.VMEM((row_count, 3 * hidden_width), arrived.dtype),
            pltpu.VMEM((row_count, 2 * hidden_width), jnp.float32),
            pltpu.VMEM((row_count, hidden_width), jnp.float32),
            pltpu.SemaphoreType.DMA((9,)),
        ],
        far_out=True,
    )


def terms_kernel(numbers, own, other, own_sides, other_sides, *terms):
    blocks = own.shape[0] // 2
    hidden_width = own_sides.shape[1] // 3
    for place, term in enumerate(terms):
        number = numbers[place]
        for first, sides in ((0, slice(0, 2 * hidden_width)), (blocks, slice(2 * hidden_width, None))):
            total = contract_rows(own[first + number], own_sides[:, sides])
            total += contract_rows(other[first + number], other_sides[:, sides])
            term[:, sides] = total.astype(term.dtype)


def local(tokens, cotangent, bucket, w_gate, w_up, w_down):
    token_count, model_width = tokens.shape
    expert_count = lax.axis_size("ep")
    capacity = max(2, 5 * token_count // (4 * expert_count))
    slot_rows = expert_count * capacity
    shard_width = w_gate.shape[1]
    hidden_width = w_gate.shape[2]
    place = lax.axis_index("fsdp")
    core = lax.bitwise_and(place, 1)
    chip = lax.shift_right_logical(place, 1)
    sizes = (expert_count, capacity)
    choice = bucket.reshape(1, token_count)

    blocked = jax.ShapeDtypeStruct(
        (slot_rows, 2 * model_width // shard_width, shard_width), tokens.dtype
    )
    packed, selector = pack_rows(functools.partial(pack_kernel, *sizes), blocked, choice, tokens, cotangent)
    packed, w_gate, w_up, w_down = lax.optimization_barrier((packed, w_gate, w_up, w_down))
    arrived = exchange(packed, expert_count)
    shard = jnp.concatenate([w_gate[0], w_up[0], w_down[0]], axis=1)
    groups, numbers = gather_weights(shard, chip, core)
    returned, sides, rows = expert_rows(arrived, groups, numbers, hidden_width)
    returned, rows, sides = lax.optimization_barrier((returned, rows, sides))
    back = exchange(returned, expert_count)

    other_rows = core_swap(rows)
    other_sides = core_swap(sides)
    targets = [(dy, dx) for dy in range(Y) for dx in range(X_HI)]
    columns = jnp.stack([chip_at(chip, dy, dx) * 2 + core for dy, dx in targets]).astype(jnp.int32)
    shape = jax.ShapeDtypeStruct((shard_width, 3 * hidden_width), tokens.dtype)
    terms = vmem_call(
        terms_kernel, [shape] * len(targets), columns, rows, other_rows, sides, other_sides
    )
    terms = dict(zip(targets, terms))

    def add(*arrays):
        return sum(array.astype(jnp.float32) for array in arrays)

    def summed(*arrays):
        return add(*arrays).astype(tokens.dtype)

    two = summed(terms[2, 0], chip_shift(terms[2, 1], 0, 1))
    across = summed(
        terms[0, 1], chip_shift(terms[1, 1], 1, 0), chip_shift(terms[3, 1], 3, 0)
    )
    total = add(
        terms[0, 0],
        chip_shift(terms[1, 0], 1, 0),
        chip_shift(terms[3, 0], 3, 0),
        chip_shift(two, 2, 0),
        chip_shift(across, 0, 1),
    )

    grads = total.astype(jnp.bfloat16)
    grad_wg = grads[None, :, :hidden_width]
    grad_wu = grads[None, :, hidden_width : 2 * hidden_width]
    grad_wd = grads[None, :, 2 * hidden_width :]
    result = jax.ShapeDtypeStruct(tokens.shape, tokens.dtype)
    outputs, input_grad = vmem_call(
        unpack_kernel,
        (result, result),
        None,
        selector,
        back,
        scratch_shapes=[
            pltpu.VMEM((2, *tokens.shape), tokens.dtype),
            pltpu.SemaphoreType.DMA((2,)),
        ],
        far_out=True,
    )
    return (outputs, input_grad, grad_wg, grad_wu, grad_wd)


def solution(mesh):
    in_specs = (
        P(("ep", "fsdp"), None),
        P(("ep", "fsdp"), None),
        P(("ep", "fsdp"), None),
        P("ep", "fsdp", None),
        P("ep", "fsdp", None),
        P("ep", "fsdp", None),
    )
    out_specs = (
        P(("ep", "fsdp"), None),
        P(("ep", "fsdp"), None),
        P("ep", "fsdp", None),
        P("ep", "fsdp", None),
        P("ep", "fsdp", None),
    )
    return jax.shard_map(local, mesh=mesh, in_specs=in_specs, out_specs=out_specs, check_vma=False)
```

```python
import functools
import jax
import jax.numpy as jnp
from jax import lax
from jax.experimental import pallas as pl
from jax.experimental.pallas import tpu as pltpu
from jax.sharding import PartitionSpec as P


def contract_rows(left_rows, right_rows):
    return lax.dot_general(
        left_rows, right_rows, (((0,), (0,)), ((), ())), preferred_element_type=jnp.float32
    )


PAIR, FIRST = 2, 11


def slot_matrix(bucket, expert_count, capacity):
    token_count = bucket.shape[1]
    labels = lax.broadcasted_iota(jnp.int32, (expert_count, token_count), 0)
    chosen = jnp.where(bucket == labels, 1.0, 0.0)
    before = lax.broadcasted_iota(jnp.int32, (token_count, token_count), 0)
    after = lax.broadcasted_iota(jnp.int32, (token_count, token_count), 1)
    earlier = jnp.dot(
        chosen.astype(jnp.bfloat16),
        jnp.where(before < after, 1.0, 0.0).astype(jnp.bfloat16),
        preferred_element_type=jnp.float32,
    )
    slot = jnp.sum(earlier * chosen, axis=0, keepdims=True).astype(jnp.int32)
    within = lax.bitwise_and(bucket, PAIR - 1)
    place = lax.rem(expert_count + FIRST * PAIR - (bucket - within), expert_count) + within
    position = place * capacity + slot
    targets = lax.broadcasted_iota(jnp.int32, (expert_count * capacity, token_count), 0)
    return jnp.where(targets == position, 1.0, 0.0).astype(jnp.bfloat16)


def vmem_call(kernel, out_shape, small, *arrays, scratch_shapes=(), far_out=False):
    vmem, far = pl.BlockSpec(memory_space=pltpu.VMEM), pl.BlockSpec(memory_space=pltpu.HBM)
    in_specs = [vmem] * len(arrays)
    if small is not None:
        in_specs = [pl.BlockSpec(memory_space=pltpu.SMEM)] + in_specs
        arrays = (small, *arrays)
    return pl.pallas_call(
        kernel,
        out_shape=jax.tree.map(lambda s: pltpu.HBM(s.shape, s.dtype), out_shape) if far_out else out_shape,
        in_specs=in_specs,
        out_specs=jax.tree.map(lambda _: far if far_out else vmem, out_shape),
        scratch_shapes=scratch_shapes,
        compiler_params=pltpu.CompilerParams(vmem_limit_bytes=20 * 1024 * 1024),
    )(*arrays)


def pack_kernel(
    expert_count,
    capacity,
    bucket,
    tokens,
    cotangent,
    packed,
    selector_out,
    choice,
    near,
    result,
    selector,
    sems,
):
    lookup = pltpu.make_async_copy(bucket, choice, sems.at[4])
    lookup.start()
    loads = [
        pltpu.make_async_copy(array, near.at[number], sems.at[number])
        for number, array in enumerate((tokens, cotangent))
    ]
    for load in loads:
        load.start()
    lookup.wait()
    selector[...] = slot_matrix(choice[...], expert_count, capacity)
    stores = [pltpu.make_async_copy(selector, selector_out, sems.at[5])]
    stores[0].start()
    lanes = packed.shape[2]
    count = packed.shape[1] // 2
    for number, load in enumerate(loads):
        load.wait()
        rows = jnp.dot(selector[...], near[number], preferred_element_type=jnp.float32)
        rows = rows.astype(packed.dtype)
        columns = [rows[:, i : i + lanes] for i in range(0, rows.shape[1], lanes)]
        part = pl.ds(number * count, count)
        result[:, part, :] = jnp.swapaxes(jnp.stack(columns, axis=0), 0, 1)
        stores.append(
            pltpu.make_async_copy(result.at[:, part], packed.at[:, part], sems.at[2 + number])
        )
        stores[-1].start()
    for store in stores:
        store.wait()


def pack_rows(kernel, out_shape, choice, tokens, cotangent):
    selector = jax.ShapeDtypeStruct((out_shape.shape[0], tokens.shape[0]), tokens.dtype)
    far = pl.BlockSpec(memory_space=pltpu.HBM)
    return pl.pallas_call(
        kernel,
        out_shape=tuple(pltpu.HBM(shape.shape, shape.dtype) for shape in (out_shape, selector)),
        in_specs=[far, far, far],
        out_specs=(far, far),
        scratch_shapes=[
            pltpu.VMEM(choice.shape, choice.dtype),
            pltpu.VMEM((2, *tokens.shape), tokens.dtype),
            pltpu.VMEM(out_shape.shape, out_shape.dtype),
            pltpu.VMEM(selector.shape, selector.dtype),
            pltpu.SemaphoreType.DMA((6,)),
        ],
        compiler_params=pltpu.CompilerParams(vmem_limit_bytes=20 * 1024 * 1024),
    )(*(pltpu.with_memory_space_constraint(a, pltpu.HBM) for a in (choice, tokens, cotangent)))


def unpack_kernel(selector, back, outputs, input_grad, results, sems):
    lanes = back.shape[2]
    count = back.shape[1] // 2
    stores = []
    for number, target in enumerate((outputs, input_grad)):
        blocks = jnp.swapaxes(back[:, number * count : (number + 1) * count], 0, 1)
        for pair in range(0, count, 2):
            rows = jnp.concatenate([blocks[pair], blocks[pair + 1]], axis=1)
            results[number, :, pair * lanes : (pair + 2) * lanes] = contract_rows(
                selector[...], rows
            ).astype(results.dtype)
        stores.append(pltpu.make_async_copy(results.at[number], target, sems.at[number]))
        stores[-1].start()
    for store in stores:
        store.wait()


def exchange(rows, expert_count):
    row_count, blocks, lanes = rows.shape
    sent = rows.reshape(expert_count, row_count // expert_count * blocks, lanes)
    order = [
        (FIRST * PAIR - back) % expert_count + within
        for back in range(0, expert_count, PAIR)
        for within in range(PAIR)
    ]
    arrived = lax.all_to_all(
        sent, "ep", split_axis=0, concat_axis=0, tiled=True, axis_index_groups=[order]
    )
    return arrived.reshape(rows.shape)


Y, X_HI = 4, 2


def core_swap(array):
    return lax.ppermute(array, "fsdp", [(f, f ^ 1) for f in range(2 * Y * X_HI)])


def chip_shift(array, dy, dx):
    pairs = []
    for y in range(Y):
        for x in range(X_HI):
            for core in range(2):
                pairs.append(
                    ((y * X_HI + x) * 2 + core, ((y + dy) % Y * X_HI + (x ^ dx)) * 2 + core)
                )
    return lax.ppermute(array, "fsdp", pairs)


def chip_at(chip, dy, dx):
    return lax.bitwise_and(chip // X_HI + dy, Y - 1) * X_HI + lax.bitwise_xor(chip % X_HI, dx)


def gather_weights(shard, chip, core):
    across, two = chip_shift(shard, 0, 1), chip_shift(shard, 2, 0)
    one, three = chip_shift(shard, 1, 0), chip_shift(shard, 3, 0)
    early = [(shard, 0, 0), (one, 3, 0), (three, 1, 0), (chip_shift(across, 1, 0), 3, 1)]
    late = [(across, 0, 1), (two, 2, 0), (chip_shift(across, 3, 0), 1, 1), (chip_shift(two, 0, 1), 2, 1)]
    groups, numbers = [], []
    for parts in (early, late):
        held = jnp.concatenate([part for part, _, _ in parts], axis=0)
        for array, side in ((held, core), (core_swap(held), 1 - core)):
            groups.append(array)
            numbers += [chip_at(chip, dy, dx) * 2 + side for _, dy, dx in parts]
    return groups, jnp.stack(numbers).astype(jnp.int32)


def expert_kernel(numbers, arrived, *refs):
    groups, (back, sides_out, rows_out) = refs[:4], refs[4:7]
    x_rows, dy_rows, y_blocks, dx_blocks, y_back, dx_back, sides, pre, grad_hidden, sems = refs[7:]
    block = arrived.shape[2]
    blocks = arrived.shape[1] // 2
    hidden_width = sides.shape[1] // 3
    stores = []

    def store(source, target):
        stores.append(pltpu.make_async_copy(source, target, sems.at[len(stores)]))
        stores[-1].start()

    pairs = [
        group.at[pl.ds(start, 2 * block)]
        for group in groups
        for start in range(0, group.shape[0], 2 * block)
    ]

    def product(rows, columns, total):
        for place, weights in enumerate(pairs):
            both = [rows[numbers[2 * place + half]] for half in range(2)]
            part = jnp.dot(
                jnp.concatenate(both, axis=1),
                weights[:, columns],
                preferred_element_type=jnp.float32,
            )
            if place == 0:
                total[...] = part
            else:
                total[...] += part

    def back_product(left, columns, result):
        left = left.T
        for place, weights in enumerate(pairs):
            part = jnp.dot(weights[:, columns], left, preferred_element_type=jnp.float32)
            part = part.T.astype(result.dtype)
            for half in range(2):
                result[numbers[2 * place + half]] = part[:, half * block : (half + 1) * block]

    gate_up, down = slice(0, 2 * hidden_width), slice(2 * hidden_width, 3 * hidden_width)
    x_rows[...] = jnp.swapaxes(arrived[:, :blocks], 0, 1)
    store(x_rows, rows_out.at[pl.ds(0, blocks)])
    dy_rows[...] = jnp.swapaxes(arrived[:, blocks:], 0, 1)
    store(dy_rows, rows_out.at[pl.ds(blocks, blocks)])

    product(x_rows, gate_up, pre)
    product(dy_rows, down, grad_hidden)
    gate_pre = pre[:, :hidden_width]
    up_proj = pre[:, hidden_width:]
    upstream = grad_hidden[...]
    sigmoid_gate = jax.nn.sigmoid(gate_pre)
    activated = gate_pre * sigmoid_gate
    hidden = (activated * up_proj).astype(sides.dtype)
    sides[:, down] = hidden
    sides[:, :hidden_width] = (
        upstream * up_proj * sigmoid_gate * (1.0 + gate_pre * (1.0 - sigmoid_gate))
    ).astype(sides.dtype)
    sides[:, hidden_width : 2 * hidden_width] = (upstream * activated).astype(sides.dtype)
    store(sides, sides_out)

    back_product(hidden, down, y_blocks)
    y_back[...] = jnp.swapaxes(y_blocks[...], 0, 1)
    store(y_back, back.at[:, pl.ds(0, blocks)])
    back_product(sides[:, gate_up], gate_up, dx_blocks)
    step = back.shape[0] // 5
    for number in range(5):
        part = pl.ds(number * step, step)
        dx_back[part] = jnp.swapaxes(dx_blocks[:, part], 0, 1)
        store(dx_back.at[part], back.at[part, pl.ds(blocks, blocks)])
    for copy in stores:
        copy.wait()


def expert_rows(arrived, groups, numbers, hidden_width):
    row_count, blocks, lanes = arrived.shape
    return vmem_call(
        expert_kernel,
        (
            jax.ShapeDtypeStruct(arrived.shape, arrived.dtype),
            jax.ShapeDtypeStruct((row_count, 3 * hidden_width), arrived.dtype),
            jax.ShapeDtypeStruct((blocks, row_count, lanes), arrived.dtype),
        ),
        numbers,
        arrived,
        *groups,
        scratch_shapes=[
            *[pltpu.VMEM((blocks // 2, row_count, lanes), arrived.dtype)] * 4,
            *[pltpu.VMEM((row_count, blocks // 2, lanes), arrived.dtype)] * 2,
            pltpu.VMEM((row_count, 3 * hidden_width), arrived.dtype),
            pltpu.VMEM((row_count, 2 * hidden_width), jnp.float32),
            pltpu.VMEM((row_count, hidden_width), jnp.float32),
            pltpu.SemaphoreType.DMA((9,)),
        ],
        far_out=True,
    )


def terms_kernel(numbers, own, other, own_sides, other_sides, *terms):
    blocks = own.shape[0] // 2
    hidden_width = own_sides.shape[1] // 3
    for place, term in enumerate(terms):
        number = numbers[place]
        for first, sides in ((0, slice(0, 2 * hidden_width)), (blocks, slice(2 * hidden_width, None))):
            total = contract_rows(own[first + number], own_sides[:, sides])
            total += contract_rows(other[first + number], other_sides[:, sides])
            term[:, sides] = total.astype(term.dtype)


def local(tokens, cotangent, bucket, w_gate, w_up, w_down):
    token_count, model_width = tokens.shape
    expert_count = lax.axis_size("ep")
    capacity = max(2, 5 * token_count // (4 * expert_count))
    slot_rows = expert_count * capacity
    shard_width = w_gate.shape[1]
    hidden_width = w_gate.shape[2]
    place = lax.axis_index("fsdp")
    core = lax.bitwise_and(place, 1)
    chip = lax.shift_right_logical(place, 1)
    sizes = (expert_count, capacity)
    choice = bucket.reshape(1, token_count)

    blocked = jax.ShapeDtypeStruct(
        (slot_rows, 2 * model_width // shard_width, shard_width), tokens.dtype
    )
    packed, selector = pack_rows(functools.partial(pack_kernel, *sizes), blocked, choice, tokens, cotangent)
    packed, w_gate, w_up, w_down = lax.optimization_barrier((packed, w_gate, w_up, w_down))
    arrived = exchange(packed, expert_count)
    shard = jnp.concatenate([w_gate[0], w_up[0], w_down[0]], axis=1)
    groups, numbers = gather_weights(shard, chip, core)
    returned, sides, rows = expert_rows(arrived, groups, numbers, hidden_width)
    returned, rows, sides = lax.optimization_barrier((returned, rows, sides))
    back = exchange(returned, expert_count)

    other_rows = core_swap(rows)
    other_sides = core_swap(sides)
    targets = [(dy, dx) for dy in range(Y) for dx in range(X_HI)]
    columns = jnp.stack([chip_at(chip, dy, dx) * 2 + core for dy, dx in targets]).astype(jnp.int32)
    shape = jax.ShapeDtypeStruct((shard_width, 3 * hidden_width), tokens.dtype)
    terms = vmem_call(
        terms_kernel, [shape] * len(targets), columns, rows, other_rows, sides, other_sides
    )
    terms = dict(zip(targets, terms))

    def add(*arrays):
        return sum(array.astype(jnp.float32) for array in arrays)

    def summed(*arrays):
        return add(*arrays).astype(tokens.dtype)

    two = summed(terms[2, 0], chip_shift(terms[2, 1], 0, 1))
    across = summed(
        terms[0, 1], chip_shift(terms[1, 1], 1, 0), chip_shift(terms[3, 1], 3, 0)
    )
    total = add(
        terms[0, 0],
        chip_shift(terms[1, 0], 1, 0),
        chip_shift(terms[3, 0], 3, 0),
        chip_shift(two, 2, 0),
        chip_shift(across, 0, 1),
    )

    grads = total.astype(jnp.bfloat16)
    grad_wg = grads[None, :, :hidden_width]
    grad_wu = grads[None, :, hidden_width : 2 * hidden_width]
    grad_wd = grads[None, :, 2 * hidden_width :]
    result = jax.ShapeDtypeStruct(tokens.shape, tokens.dtype)
    outputs, input_grad = vmem_call(
        unpack_kernel,
        (result, result),
        None,
        selector,
        back,
        scratch_shapes=[
            pltpu.VMEM((2, *tokens.shape), tokens.dtype),
            pltpu.SemaphoreType.DMA((2,)),
        ],
        far_out=True,
    )
    return (outputs, input_grad, grad_wg, grad_wu, grad_wd)


def solution(mesh):
    in_specs = (
        P(("ep", "fsdp"), None),
        P(("ep", "fsdp"), None),
        P(("ep", "fsdp"), None),
        P("ep", "fsdp", None),
        P("ep", "fsdp", None),
        P("ep", "fsdp", None),
    )
    out_specs = (
        P(("ep", "fsdp"), None),
        P(("ep", "fsdp"), None),
        P("ep", "fsdp", None),
        P("ep", "fsdp", None),
        P("ep", "fsdp", None),
    )
    return jax.shard_map(local, mesh=mesh, in_specs=in_specs, out_specs=out_specs, check_vma=False)
```

```python
import functools
import jax
import jax.numpy as jnp
from jax import lax
from jax.experimental import pallas as pl
from jax.experimental.pallas import tpu as pltpu
from jax.sharding import PartitionSpec as P


def contract_rows(left_rows, right_rows):
    return lax.dot_general(
        left_rows, right_rows, (((0,), (0,)), ((), ())), preferred_element_type=jnp.float32
    )


PAIR, FIRST = 2, 11


def slot_matrix(bucket, expert_count, capacity):
    token_count = bucket.shape[1]
    labels = lax.broadcasted_iota(jnp.int32, (expert_count, token_count), 0)
    chosen = jnp.where(bucket == labels, 1.0, 0.0)
    before = lax.broadcasted_iota(jnp.int32, (token_count, token_count), 0)
    after = lax.broadcasted_iota(jnp.int32, (token_count, token_count), 1)
    earlier = jnp.dot(
        chosen.astype(jnp.bfloat16),
        jnp.where(before < after, 1.0, 0.0).astype(jnp.bfloat16),
        preferred_element_type=jnp.float32,
    )
    slot = jnp.sum(earlier * chosen, axis=0, keepdims=True).astype(jnp.int32)
    within = lax.bitwise_and(bucket, PAIR - 1)
    place = lax.rem(expert_count + FIRST * PAIR - (bucket - within), expert_count) + within
    position = place * capacity + slot
    targets = lax.broadcasted_iota(jnp.int32, (expert_count * capacity, token_count), 0)
    return jnp.where(targets == position, 1.0, 0.0).astype(jnp.bfloat16)


def vmem_call(kernel, out_shape, small, *arrays, scratch_shapes=(), far_out=False):
    vmem, far = pl.BlockSpec(memory_space=pltpu.VMEM), pl.BlockSpec(memory_space=pltpu.HBM)
    in_specs = [vmem] * len(arrays)
    if small is not None:
        in_specs = [pl.BlockSpec(memory_space=pltpu.SMEM)] + in_specs
        arrays = (small, *arrays)
    return pl.pallas_call(
        kernel,
        out_shape=jax.tree.map(lambda s: pltpu.HBM(s.shape, s.dtype), out_shape) if far_out else out_shape,
        in_specs=in_specs,
        out_specs=jax.tree.map(lambda _: far if far_out else vmem, out_shape),
        scratch_shapes=scratch_shapes,
        compiler_params=pltpu.CompilerParams(vmem_limit_bytes=20 * 1024 * 1024),
    )(*arrays)


def pack_kernel(
    expert_count,
    capacity,
    bucket,
    tokens,
    cotangent,
    packed,
    selector_out,
    choice,
    near,
    result,
    selector,
    sems,
):
    lookup = pltpu.make_async_copy(bucket, choice, sems.at[4])
    lookup.start()
    loads = [
        pltpu.make_async_copy(array, near.at[number], sems.at[number])
        for number, array in enumerate((tokens, cotangent))
    ]
    for load in loads:
        load.start()
    lookup.wait()
    selector[...] = slot_matrix(choice[...], expert_count, capacity)
    stores = [pltpu.make_async_copy(selector, selector_out, sems.at[5])]
    stores[0].start()
    lanes = packed.shape[2]
    count = packed.shape[1] // 2
    for number, load in enumerate(loads):
        load.wait()
        rows = jnp.dot(selector[...], near[number], preferred_element_type=jnp.float32)
        rows = rows.astype(packed.dtype)
        columns = [rows[:, i : i + lanes] for i in range(0, rows.shape[1], lanes)]
        part = pl.ds(number * count, count)
        result[:, part, :] = jnp.swapaxes(jnp.stack(columns, axis=0), 0, 1)
        stores.append(
            pltpu.make_async_copy(result.at[:, part], packed.at[:, part], sems.at[2 + number])
        )
        stores[-1].start()
    for store in stores:
        store.wait()


def pack_rows(kernel, out_shape, choice, tokens, cotangent):
    selector = jax.ShapeDtypeStruct((out_shape.shape[0], tokens.shape[0]), tokens.dtype)
    far = pl.BlockSpec(memory_space=pltpu.HBM)
    return pl.pallas_call(
        kernel,
        out_shape=tuple(pltpu.HBM(shape.shape, shape.dtype) for shape in (out_shape, selector)),
        in_specs=[far, far, far],
        out_specs=(far, far),
        scratch_shapes=[
            pltpu.VMEM(choice.shape, choice.dtype),
            pltpu.VMEM((2, *tokens.shape), tokens.dtype),
            pltpu.VMEM(out_shape.shape, out_shape.dtype),
            pltpu.VMEM(selector.shape, selector.dtype),
            pltpu.SemaphoreType.DMA((6,)),
        ],
        compiler_params=pltpu.CompilerParams(vmem_limit_bytes=20 * 1024 * 1024),
    )(*(pltpu.with_memory_space_constraint(a, pltpu.HBM) for a in (choice, tokens, cotangent)))


def unpack_kernel(selector, back, outputs, input_grad, results, sems):
    lanes = back.shape[2]
    count = back.shape[1] // 2
    stores = []
    for number, target in enumerate((outputs, input_grad)):
        blocks = jnp.swapaxes(back[:, number * count : (number + 1) * count], 0, 1)
        for pair in range(0, count, 2):
            rows = jnp.concatenate([blocks[pair], blocks[pair + 1]], axis=1)
            results[number, :, pair * lanes : (pair + 2) * lanes] = contract_rows(
                selector[...], rows
            ).astype(results.dtype)
        stores.append(pltpu.make_async_copy(results.at[number], target, sems.at[number]))
        stores[-1].start()
    for store in stores:
        store.wait()


def exchange(rows, expert_count):
    row_count, blocks, lanes = rows.shape
    sent = rows.reshape(expert_count, row_count // expert_count * blocks, lanes)
    order = [
        (FIRST * PAIR - back) % expert_count + within
        for back in range(0, expert_count, PAIR)
        for within in range(PAIR)
    ]
    arrived = lax.all_to_all(
        sent, "ep", split_axis=0, concat_axis=0, tiled=True, axis_index_groups=[order]
    )
    return arrived.reshape(rows.shape)


Y, X_HI = 4, 2


def core_swap(array):
    return lax.ppermute(array, "fsdp", [(f, f ^ 1) for f in range(2 * Y * X_HI)])


def chip_shift(array, dy, dx):
    pairs = []
    for y in range(Y):
        for x in range(X_HI):
            for core in range(2):
                pairs.append(
                    ((y * X_HI + x) * 2 + core, ((y + dy) % Y * X_HI + (x ^ dx)) * 2 + core)
                )
    return lax.ppermute(array, "fsdp", pairs)


def chip_at(chip, dy, dx):
    return lax.bitwise_and(chip // X_HI + dy, Y - 1) * X_HI + lax.bitwise_xor(chip % X_HI, dx)


def gather_weights(shard, chip, core):
    across, two = chip_shift(shard, 0, 1), chip_shift(shard, 2, 0)
    one, three = chip_shift(shard, 1, 0), chip_shift(shard, 3, 0)
    early = [(shard, 0, 0), (one, 3, 0), (three, 1, 0), (chip_shift(across, 1, 0), 3, 1)]
    late = [(across, 0, 1), (two, 2, 0), (chip_shift(across, 3, 0), 1, 1), (chip_shift(two, 0, 1), 2, 1)]
    groups, numbers = [], []
    for parts in (early, late):
        held = jnp.concatenate([part for part, _, _ in parts], axis=0)
        for array, side in ((held, core), (core_swap(held), 1 - core)):
            groups.append(array)
            numbers += [chip_at(chip, dy, dx) * 2 + side for _, dy, dx in parts]
    return groups, jnp.stack(numbers).astype(jnp.int32)


def expert_kernel(numbers, arrived, *refs):
    groups, (back, sides_out, rows_out) = refs[:4], refs[4:7]
    x_rows, dy_rows, y_blocks, dx_blocks, y_back, dx_back, sides, pre, grad_hidden, sems = refs[7:]
    block = arrived.shape[2]
    blocks = arrived.shape[1] // 2
    hidden_width = sides.shape[1] // 3
    stores = []

    def store(source, target):
        stores.append(pltpu.make_async_copy(source, target, sems.at[len(stores)]))
        stores[-1].start()

    pairs = [
        group.at[pl.ds(start, 2 * block)]
        for group in groups
        for start in range(0, group.shape[0], 2 * block)
    ]

    def product(rows, columns, total):
        for place, weights in enumerate(pairs):
            both = [rows[numbers[2 * place + half]] for half in range(2)]
            part = jnp.dot(
                jnp.concatenate(both, axis=1),
                weights[:, columns],
                preferred_element_type=jnp.float32,
            )
            if place == 0:
                total[...] = part
            else:
                total[...] += part

    def back_product(left, columns, result):
        left = left.T
        for place, weights in enumerate(pairs):
            part = jnp.dot(weights[:, columns], left, preferred_element_type=jnp.float32)
            part = part.T.astype(result.dtype)
            for half in range(2):
                result[numbers[2 * place + half]] = part[:, half * block : (half + 1) * block]

    gate_up, down = slice(0, 2 * hidden_width), slice(2 * hidden_width, 3 * hidden_width)
    x_rows[...] = jnp.swapaxes(arrived[:, :blocks], 0, 1)
    store(x_rows, rows_out.at[pl.ds(0, blocks)])
    dy_rows[...] = jnp.swapaxes(arrived[:, blocks:], 0, 1)
    store(dy_rows, rows_out.at[pl.ds(blocks, blocks)])

    product(x_rows, gate_up, pre)
    product(dy_rows, down, grad_hidden)
    gate_pre = pre[:, :hidden_width]
    up_proj = pre[:, hidden_width:]
    upstream = grad_hidden[...]
    sigmoid_gate = jax.nn.sigmoid(gate_pre)
    activated = gate_pre * sigmoid_gate
    hidden = (activated * up_proj).astype(sides.dtype)
    sides[:, down] = hidden
    sides[:, :hidden_width] = (
        upstream * up_proj * sigmoid_gate * (1.0 + gate_pre * (1.0 - sigmoid_gate))
    ).astype(sides.dtype)
    sides[:, hidden_width : 2 * hidden_width] = (upstream * activated).astype(sides.dtype)
    store(sides, sides_out)

    back_product(hidden, down, y_blocks)
    y_back[...] = jnp.swapaxes(y_blocks[...], 0, 1)
    store(y_back, back.at[:, pl.ds(0, blocks)])
    back_product(sides[:, gate_up], gate_up, dx_blocks)
    step = back.shape[0] // 5
    for number in range(5):
        part = pl.ds(number * step, step)
        dx_back[part] = jnp.swapaxes(dx_blocks[:, part], 0, 1)
        store(dx_back.at[part], back.at[part, pl.ds(blocks, blocks)])
    for copy in stores:
        copy.wait()


def expert_rows(arrived, groups, numbers, hidden_width):
    row_count, blocks, lanes = arrived.shape
    return vmem_call(
        expert_kernel,
        (
            jax.ShapeDtypeStruct(arrived.shape, arrived.dtype),
            jax.ShapeDtypeStruct((row_count, 3 * hidden_width), arrived.dtype),
            jax.ShapeDtypeStruct((blocks, row_count, lanes), arrived.dtype),
        ),
        numbers,
        arrived,
        *groups,
        scratch_shapes=[
            *[pltpu.VMEM((blocks // 2, row_count, lanes), arrived.dtype)] * 4,
            *[pltpu.VMEM((row_count, blocks // 2, lanes), arrived.dtype)] * 2,
            pltpu.VMEM((row_count, 3 * hidden_width), arrived.dtype),
            pltpu.VMEM((row_count, 2 * hidden_width), jnp.float32),
            pltpu.VMEM((row_count, hidden_width), jnp.float32),
            pltpu.SemaphoreType.DMA((9,)),
        ],
        far_out=True,
    )


def terms_kernel(numbers, own, other, own_sides, other_sides, *terms):
    blocks = own.shape[0] // 2
    hidden_width = own_sides.shape[1] // 3
    for place, term in enumerate(terms):
        number = numbers[place]
        for first, sides in ((0, slice(0, 2 * hidden_width)), (blocks, slice(2 * hidden_width, None))):
            total = contract_rows(own[first + number], own_sides[:, sides])
            total += contract_rows(other[first + number], other_sides[:, sides])
            term[:, sides] = total.astype(term.dtype)


def local(tokens, cotangent, bucket, w_gate, w_up, w_down):
    token_count, model_width = tokens.shape
    expert_count = lax.axis_size("ep")
    capacity = max(2, 5 * token_count // (4 * expert_count))
    slot_rows = expert_count * capacity
    shard_width = w_gate.shape[1]
    hidden_width = w_gate.shape[2]
    place = lax.axis_index("fsdp")
    core = lax.bitwise_and(place, 1)
    chip = lax.shift_right_logical(place, 1)
    sizes = (expert_count, capacity)
    choice = bucket.reshape(1, token_count)

    blocked = jax.ShapeDtypeStruct(
        (slot_rows, 2 * model_width // shard_width, shard_width), tokens.dtype
    )
    packed, selector = pack_rows(functools.partial(pack_kernel, *sizes), blocked, choice, tokens, cotangent)
    packed, w_gate, w_up, w_down = lax.optimization_barrier((packed, w_gate, w_up, w_down))
    arrived = exchange(packed, expert_count)
    shard = jnp.concatenate([w_gate[0], w_up[0], w_down[0]], axis=1)
    groups, numbers = gather_weights(shard, chip, core)
    returned, sides, rows = expert_rows(arrived, groups, numbers, hidden_width)
    returned, rows, sides = lax.optimization_barrier((returned, rows, sides))
    back = exchange(returned, expert_count)

    other_rows = core_swap(rows)
    other_sides = core_swap(sides)
    targets = [(dy, dx) for dy in range(Y) for dx in range(X_HI)]
    columns = jnp.stack([chip_at(chip, dy, dx) * 2 + core for dy, dx in targets]).astype(jnp.int32)
    shape = jax.ShapeDtypeStruct((shard_width, 3 * hidden_width), tokens.dtype)
    terms = vmem_call(
        terms_kernel, [shape] * len(targets), columns, rows, other_rows, sides, other_sides
    )
    terms = dict(zip(targets, terms))

    def add(*arrays):
        return sum(array.astype(jnp.float32) for array in arrays)

    def summed(*arrays):
        return add(*arrays).astype(tokens.dtype)

    crossed, one, three = lax.optimization_barrier(
        (chip_shift(terms[2, 1], 0, 1), terms[1, 0], terms[3, 0])
    )
    two = summed(terms[2, 0], crossed)
    across = summed(
        terms[0, 1], chip_shift(terms[1, 1], 1, 0), chip_shift(terms[3, 1], 3, 0)
    )
    total = add(
        terms[0, 0],
        chip_shift(one, 1, 0),
        chip_shift(three, 3, 0),
        chip_shift(two, 2, 0),
        chip_shift(across, 0, 1),
    )

    grads = total.astype(jnp.bfloat16)
    grad_wg = grads[None, :, :hidden_width]
    grad_wu = grads[None, :, hidden_width : 2 * hidden_width]
    grad_wd = grads[None, :, 2 * hidden_width :]
    result = jax.ShapeDtypeStruct(tokens.shape, tokens.dtype)
    outputs, input_grad = vmem_call(
        unpack_kernel,
        (result, result),
        None,
        selector,
        back,
        scratch_shapes=[
            pltpu.VMEM((2, *tokens.shape), tokens.dtype),
            pltpu.SemaphoreType.DMA((2,)),
        ],
        far_out=True,
    )
    return (outputs, input_grad, grad_wg, grad_wu, grad_wd)


def solution(mesh):
    in_specs = (
        P(("ep", "fsdp"), None),
        P(("ep", "fsdp"), None),
        P(("ep", "fsdp"), None),
        P("ep", "fsdp", None),
        P("ep", "fsdp", None),
        P("ep", "fsdp", None),
    )
    out_specs = (
        P(("ep", "fsdp"), None),
        P(("ep", "fsdp"), None),
        P("ep", "fsdp", None),
        P("ep", "fsdp", None),
        P("ep", "fsdp", None),
    )
    return jax.shard_map(local, mesh=mesh, in_specs=in_specs, out_specs=out_specs, check_vma=False)
```

```python
import functools
import jax
import jax.numpy as jnp
from jax import lax
from jax.experimental import pallas as pl
from jax.experimental.pallas import tpu as pltpu
from jax.sharding import PartitionSpec as P


def contract_rows(left_rows, right_rows):
    return lax.dot_general(
        left_rows, right_rows, (((0,), (0,)), ((), ())), preferred_element_type=jnp.float32
    )


PAIR, FIRST = 2, 11


def slot_matrix(bucket, expert_count, capacity):
    token_count = bucket.shape[1]
    labels = lax.broadcasted_iota(jnp.int32, (expert_count, token_count), 0)
    chosen = jnp.where(bucket == labels, 1.0, 0.0)
    before = lax.broadcasted_iota(jnp.int32, (token_count, token_count), 0)
    after = lax.broadcasted_iota(jnp.int32, (token_count, token_count), 1)
    earlier = jnp.dot(
        chosen.astype(jnp.bfloat16),
        jnp.where(before < after, 1.0, 0.0).astype(jnp.bfloat16),
        preferred_element_type=jnp.float32,
    )
    slot = jnp.sum(earlier * chosen, axis=0, keepdims=True).astype(jnp.int32)
    within = lax.bitwise_and(bucket, PAIR - 1)
    place = lax.rem(expert_count + FIRST * PAIR - (bucket - within), expert_count) + within
    position = place * capacity + slot
    targets = lax.broadcasted_iota(jnp.int32, (expert_count * capacity, token_count), 0)
    return jnp.where(targets == position, 1.0, 0.0).astype(jnp.bfloat16)


def vmem_call(kernel, out_shape, small, *arrays, scratch_shapes=(), far_out=False):
    vmem, far = pl.BlockSpec(memory_space=pltpu.VMEM), pl.BlockSpec(memory_space=pltpu.HBM)
    in_specs = [vmem] * len(arrays)
    if small is not None:
        in_specs = [pl.BlockSpec(memory_space=pltpu.SMEM)] + in_specs
        arrays = (small, *arrays)
    return pl.pallas_call(
        kernel,
        out_shape=jax.tree.map(lambda s: pltpu.HBM(s.shape, s.dtype), out_shape) if far_out else out_shape,
        in_specs=in_specs,
        out_specs=jax.tree.map(lambda _: far if far_out else vmem, out_shape),
        scratch_shapes=scratch_shapes,
        compiler_params=pltpu.CompilerParams(vmem_limit_bytes=20 * 1024 * 1024),
    )(*arrays)


def pack_kernel(
    expert_count,
    capacity,
    bucket,
    tokens,
    cotangent,
    packed,
    selector_out,
    choice,
    near,
    result,
    selector,
    sems,
):
    lookup = pltpu.make_async_copy(bucket, choice, sems.at[4])
    lookup.start()
    loads = [
        pltpu.make_async_copy(array, near.at[number], sems.at[number])
        for number, array in enumerate((tokens, cotangent))
    ]
    for load in loads:
        load.start()
    lookup.wait()
    selector[...] = slot_matrix(choice[...], expert_count, capacity)
    stores = [pltpu.make_async_copy(selector, selector_out, sems.at[5])]
    stores[0].start()
    lanes = packed.shape[2]
    count = packed.shape[1] // 2
    for number, load in enumerate(loads):
        load.wait()
        rows = jnp.dot(selector[...], near[number], preferred_element_type=jnp.float32)
        rows = rows.astype(packed.dtype)
        columns = [rows[:, i : i + lanes] for i in range(0, rows.shape[1], lanes)]
        part = pl.ds(number * count, count)
        result[:, part, :] = jnp.swapaxes(jnp.stack(columns, axis=0), 0, 1)
        stores.append(
            pltpu.make_async_copy(result.at[:, part], packed.at[:, part], sems.at[2 + number])
        )
        stores[-1].start()
    for store in stores:
        store.wait()


def pack_rows(kernel, out_shape, choice, tokens, cotangent):
    selector = jax.ShapeDtypeStruct((out_shape.shape[0], tokens.shape[0]), tokens.dtype)
    far = pl.BlockSpec(memory_space=pltpu.HBM)
    return pl.pallas_call(
        kernel,
        out_shape=tuple(pltpu.HBM(shape.shape, shape.dtype) for shape in (out_shape, selector)),
        in_specs=[far, far, far],
        out_specs=(far, far),
        scratch_shapes=[
            pltpu.VMEM(choice.shape, choice.dtype),
            pltpu.VMEM((2, *tokens.shape), tokens.dtype),
            pltpu.VMEM(out_shape.shape, out_shape.dtype),
            pltpu.VMEM(selector.shape, selector.dtype),
            pltpu.SemaphoreType.DMA((6,)),
        ],
        compiler_params=pltpu.CompilerParams(vmem_limit_bytes=20 * 1024 * 1024),
    )(*(pltpu.with_memory_space_constraint(a, pltpu.HBM) for a in (choice, tokens, cotangent)))


def unpack_kernel(selector, back, outputs, input_grad, results, sems):
    lanes = back.shape[2]
    count = back.shape[1] // 2
    stores = []
    for number, target in enumerate((outputs, input_grad)):
        blocks = jnp.swapaxes(back[:, number * count : (number + 1) * count], 0, 1)
        for pair in range(0, count, 2):
            rows = jnp.concatenate([blocks[pair], blocks[pair + 1]], axis=1)
            results[number, :, pair * lanes : (pair + 2) * lanes] = contract_rows(
                selector[...], rows
            ).astype(results.dtype)
        stores.append(pltpu.make_async_copy(results.at[number], target, sems.at[number]))
        stores[-1].start()
    for store in stores:
        store.wait()


def exchange(rows, expert_count):
    row_count, blocks, lanes = rows.shape
    sent = rows.reshape(expert_count, row_count // expert_count * blocks, lanes)
    order = [
        (FIRST * PAIR - back) % expert_count + within
        for back in range(0, expert_count, PAIR)
        for within in range(PAIR)
    ]
    arrived = lax.all_to_all(
        sent, "ep", split_axis=0, concat_axis=0, tiled=True, axis_index_groups=[order]
    )
    return arrived.reshape(rows.shape)


Y, X_HI = 4, 2


def core_swap(array):
    return lax.ppermute(array, "fsdp", [(f, f ^ 1) for f in range(2 * Y * X_HI)])


def chip_shift(array, dy, dx):
    pairs = []
    for y in range(Y):
        for x in range(X_HI):
            for core in range(2):
                pairs.append(
                    ((y * X_HI + x) * 2 + core, ((y + dy) % Y * X_HI + (x ^ dx)) * 2 + core)
                )
    return lax.ppermute(array, "fsdp", pairs)


def chip_at(chip, dy, dx):
    return lax.bitwise_and(chip // X_HI + dy, Y - 1) * X_HI + lax.bitwise_xor(chip % X_HI, dx)


def gather_weights(shard, chip, core):
    across, two = chip_shift(shard, 0, 1), chip_shift(shard, 2, 0)
    one, three = chip_shift(shard, 1, 0), chip_shift(shard, 3, 0)
    early = [(shard, 0, 0), (one, 3, 0), (three, 1, 0), (chip_shift(across, 1, 0), 3, 1)]
    late = [(across, 0, 1), (two, 2, 0), (chip_shift(across, 3, 0), 1, 1), (chip_shift(two, 0, 1), 2, 1)]
    groups, numbers = [], []
    for parts in (early, late):
        held = jnp.concatenate([part for part, _, _ in parts], axis=0)
        for array, side in ((held, core), (core_swap(held), 1 - core)):
            groups.append(array)
            numbers += [chip_at(chip, dy, dx) * 2 + side for _, dy, dx in parts]
    return groups, jnp.stack(numbers).astype(jnp.int32)


def expert_kernel(numbers, arrived, *refs):
    groups, (back, sides_out, rows_out) = refs[:4], refs[4:7]
    x_rows, dy_rows, y_blocks, dx_blocks, y_back, dx_back, sides, pre, grad_hidden, sems = refs[7:]
    block = arrived.shape[2]
    blocks = arrived.shape[1] // 2
    hidden_width = sides.shape[1] // 3
    stores = []

    def store(source, target):
        stores.append(pltpu.make_async_copy(source, target, sems.at[len(stores)]))
        stores[-1].start()

    pairs = [
        group.at[pl.ds(start, 2 * block)]
        for group in groups
        for start in range(0, group.shape[0], 2 * block)
    ]

    def product(rows, columns, total):
        for place, weights in enumerate(pairs):
            both = [rows[numbers[2 * place + half]] for half in range(2)]
            part = jnp.dot(
                jnp.concatenate(both, axis=1),
                weights[:, columns],
                preferred_element_type=jnp.float32,
            )
            if place == 0:
                total[...] = part
            else:
                total[...] += part

    def back_product(left, columns, result):
        left = left.T
        for place, weights in enumerate(pairs):
            part = jnp.dot(weights[:, columns], left, preferred_element_type=jnp.float32)
            part = part.T.astype(result.dtype)
            for half in range(2):
                result[numbers[2 * place + half]] = part[:, half * block : (half + 1) * block]

    gate_up, down = slice(0, 2 * hidden_width), slice(2 * hidden_width, 3 * hidden_width)
    x_rows[...] = jnp.swapaxes(arrived[:, :blocks], 0, 1)
    store(x_rows, rows_out.at[pl.ds(0, blocks)])
    dy_rows[...] = jnp.swapaxes(arrived[:, blocks:], 0, 1)
    store(dy_rows, rows_out.at[pl.ds(blocks, blocks)])

    product(x_rows, gate_up, pre)
    product(dy_rows, down, grad_hidden)
    gate_pre = pre[:, :hidden_width]
    up_proj = pre[:, hidden_width:]
    upstream = grad_hidden[...]
    sigmoid_gate = jax.nn.sigmoid(gate_pre)
    activated = gate_pre * sigmoid_gate
    hidden = (activated * up_proj).astype(sides.dtype)
    sides[:, down] = hidden
    sides[:, :hidden_width] = (
        upstream * up_proj * sigmoid_gate * (1.0 + gate_pre * (1.0 - sigmoid_gate))
    ).astype(sides.dtype)
    sides[:, hidden_width : 2 * hidden_width] = (upstream * activated).astype(sides.dtype)
    store(sides, sides_out)

    back_product(hidden, down, y_blocks)
    y_back[...] = jnp.swapaxes(y_blocks[...], 0, 1)
    store(y_back, back.at[:, pl.ds(0, blocks)])
    back_product(sides[:, gate_up], gate_up, dx_blocks)
    step = back.shape[0] // 5
    for number in range(5):
        part = pl.ds(number * step, step)
        dx_back[part] = jnp.swapaxes(dx_blocks[:, part], 0, 1)
        store(dx_back.at[part], back.at[part, pl.ds(blocks, blocks)])
    for copy in stores:
        copy.wait()


def expert_rows(arrived, groups, numbers, hidden_width):
    row_count, blocks, lanes = arrived.shape
    return vmem_call(
        expert_kernel,
        (
            jax.ShapeDtypeStruct(arrived.shape, arrived.dtype),
            jax.ShapeDtypeStruct((row_count, 3 * hidden_width), arrived.dtype),
            jax.ShapeDtypeStruct((blocks, row_count, lanes), arrived.dtype),
        ),
        numbers,
        arrived,
        *groups,
        scratch_shapes=[
            *[pltpu.VMEM((blocks // 2, row_count, lanes), arrived.dtype)] * 4,
            *[pltpu.VMEM((row_count, blocks // 2, lanes), arrived.dtype)] * 2,
            pltpu.VMEM((row_count, 3 * hidden_width), arrived.dtype),
            pltpu.VMEM((row_count, 2 * hidden_width), jnp.float32),
            pltpu.VMEM((row_count, hidden_width), jnp.float32),
            pltpu.SemaphoreType.DMA((9,)),
        ],
        far_out=True,
    )


def terms_kernel(numbers, own, other, own_sides, other_sides, *terms):
    blocks = own.shape[0] // 2
    hidden_width = own_sides.shape[1] // 3
    for place, term in enumerate(terms):
        number = numbers[place]
        for first, sides in ((0, slice(0, 2 * hidden_width)), (blocks, slice(2 * hidden_width, None))):
            total = contract_rows(own[first + number], own_sides[:, sides])
            total += contract_rows(other[first + number], other_sides[:, sides])
            term[:, sides] = total.astype(term.dtype)


def local(tokens, cotangent, bucket, w_gate, w_up, w_down):
    token_count, model_width = tokens.shape
    expert_count = lax.axis_size("ep")
    capacity = max(2, 5 * token_count // (4 * expert_count))
    slot_rows = expert_count * capacity
    shard_width = w_gate.shape[1]
    hidden_width = w_gate.shape[2]
    place = lax.axis_index("fsdp")
    core = lax.bitwise_and(place, 1)
    chip = lax.shift_right_logical(place, 1)
    sizes = (expert_count, capacity)
    choice = bucket.reshape(1, token_count)

    blocked = jax.ShapeDtypeStruct(
        (slot_rows, 2 * model_width // shard_width, shard_width), tokens.dtype
    )
    packed, selector = pack_rows(functools.partial(pack_kernel, *sizes), blocked, choice, tokens, cotangent)
    packed, w_gate, w_up, w_down = lax.optimization_barrier((packed, w_gate, w_up, w_down))
    arrived = exchange(packed, expert_count)
    shard = jnp.concatenate([w_gate[0], w_up[0], w_down[0]], axis=1)
    groups, numbers = gather_weights(shard, chip, core)
    returned, sides, rows = expert_rows(arrived, groups, numbers, hidden_width)
    returned, rows, sides = lax.optimization_barrier((returned, rows, sides))
    back = exchange(returned, expert_count)

    other_rows = core_swap(rows)
    other_sides = core_swap(sides)
    targets = [(dy, dx) for dy in range(Y) for dx in range(X_HI)]
    columns = jnp.stack([chip_at(chip, dy, dx) * 2 + core for dy, dx in targets]).astype(jnp.int32)
    shape = jax.ShapeDtypeStruct((shard_width, 3 * hidden_width), tokens.dtype)
    terms = vmem_call(
        terms_kernel, [shape] * len(targets), columns, rows, other_rows, sides, other_sides
    )
    terms = dict(zip(targets, terms))

    def add(*arrays):
        return sum(array.astype(jnp.float32) for array in arrays)

    def summed(*arrays):
        return add(*arrays).astype(tokens.dtype)

    near, far = chip_shift(terms[1, 1], 1, 0), chip_shift(terms[3, 1], 3, 0)
    one, three = chip_shift(terms[1, 0], 1, 0), chip_shift(terms[3, 0], 3, 0)
    two = summed(terms[2, 0], chip_shift(terms[2, 1], 0, 1))
    across = summed(terms[0, 1], near, far)
    partial = add(terms[0, 0], one, three)
    last = add(chip_shift(two, 2, 0), chip_shift(across, 0, 1))
    last, partial = lax.optimization_barrier((last, partial))
    total = last + partial

    grads = total.astype(jnp.bfloat16)
    grad_wg = grads[None, :, :hidden_width]
    grad_wu = grads[None, :, hidden_width : 2 * hidden_width]
    grad_wd = grads[None, :, 2 * hidden_width :]
    result = jax.ShapeDtypeStruct(tokens.shape, tokens.dtype)
    outputs, input_grad = vmem_call(
        unpack_kernel,
        (result, result),
        None,
        selector,
        back,
        scratch_shapes=[
            pltpu.VMEM((2, *tokens.shape), tokens.dtype),
            pltpu.SemaphoreType.DMA((2,)),
        ],
        far_out=True,
    )
    return (outputs, input_grad, grad_wg, grad_wu, grad_wd)


def solution(mesh):
    in_specs = (
        P(("ep", "fsdp"), None),
        P(("ep", "fsdp"), None),
        P(("ep", "fsdp"), None),
        P("ep", "fsdp", None),
        P("ep", "fsdp", None),
        P("ep", "fsdp", None),
    )
    out_specs = (
        P(("ep", "fsdp"), None),
        P(("ep", "fsdp"), None),
        P("ep", "fsdp", None),
        P("ep", "fsdp", None),
        P("ep", "fsdp", None),
    )
    return jax.shard_map(local, mesh=mesh, in_specs=in_specs, out_specs=out_specs, check_vma=False)
```

```python
import functools
import jax
import jax.numpy as jnp
from jax import lax
from jax.experimental import pallas as pl
from jax.experimental.pallas import tpu as pltpu
from jax.sharding import PartitionSpec as P


def contract_rows(left_rows, right_rows):
    return lax.dot_general(
        left_rows, right_rows, (((0,), (0,)), ((), ())), preferred_element_type=jnp.float32
    )


PAIR, FIRST = 2, 9


def slot_matrix(bucket, expert_count, capacity):
    token_count = bucket.shape[1]
    labels = lax.broadcasted_iota(jnp.int32, (expert_count, token_count), 0)
    chosen = jnp.where(bucket == labels, 1.0, 0.0)
    before = lax.broadcasted_iota(jnp.int32, (token_count, token_count), 0)
    after = lax.broadcasted_iota(jnp.int32, (token_count, token_count), 1)
    earlier = jnp.dot(
        chosen.astype(jnp.bfloat16),
        jnp.where(before < after, 1.0, 0.0).astype(jnp.bfloat16),
        preferred_element_type=jnp.float32,
    )
    slot = jnp.sum(earlier * chosen, axis=0, keepdims=True).astype(jnp.int32)
    within = lax.bitwise_and(bucket, PAIR - 1)
    place = lax.rem(expert_count + FIRST * PAIR - (bucket - within), expert_count) + within
    position = place * capacity + slot
    targets = lax.broadcasted_iota(jnp.int32, (expert_count * capacity, token_count), 0)
    return jnp.where(targets == position, 1.0, 0.0).astype(jnp.bfloat16)


def vmem_call(kernel, out_shape, small, *arrays, scratch_shapes=(), far_out=False):
    vmem, far = pl.BlockSpec(memory_space=pltpu.VMEM), pl.BlockSpec(memory_space=pltpu.HBM)
    in_specs = [vmem] * len(arrays)
    if small is not None:
        in_specs = [pl.BlockSpec(memory_space=pltpu.SMEM)] + in_specs
        arrays = (small, *arrays)
    return pl.pallas_call(
        kernel,
        out_shape=jax.tree.map(lambda s: pltpu.HBM(s.shape, s.dtype), out_shape) if far_out else out_shape,
        in_specs=in_specs,
        out_specs=jax.tree.map(lambda _: far if far_out else vmem, out_shape),
        scratch_shapes=scratch_shapes,
        compiler_params=pltpu.CompilerParams(vmem_limit_bytes=20 * 1024 * 1024),
    )(*arrays)


def pack_kernel(
    expert_count,
    capacity,
    bucket,
    tokens,
    cotangent,
    packed,
    selector_out,
    choice,
    near,
    result,
    selector,
    sems,
):
    lookup = pltpu.make_async_copy(bucket, choice, sems.at[4])
    lookup.start()
    loads = [
        pltpu.make_async_copy(array, near.at[number], sems.at[number])
        for number, array in enumerate((tokens, cotangent))
    ]
    for load in loads:
        load.start()
    lookup.wait()
    selector[...] = slot_matrix(choice[...], expert_count, capacity)
    stores = [pltpu.make_async_copy(selector, selector_out, sems.at[5])]
    stores[0].start()
    lanes = packed.shape[2]
    count = packed.shape[1] // 2
    for number, load in enumerate(loads):
        load.wait()
        rows = jnp.dot(selector[...], near[number], preferred_element_type=jnp.float32)
        rows = rows.astype(packed.dtype)
        columns = [rows[:, i : i + lanes] for i in range(0, rows.shape[1], lanes)]
        part = pl.ds(number * count, count)
        result[:, part, :] = jnp.swapaxes(jnp.stack(columns, axis=0), 0, 1)
        stores.append(
            pltpu.make_async_copy(result.at[:, part], packed.at[:, part], sems.at[2 + number])
        )
        stores[-1].start()
    for store in stores:
        store.wait()


def pack_rows(kernel, out_shape, choice, tokens, cotangent):
    selector = jax.ShapeDtypeStruct((out_shape.shape[0], tokens.shape[0]), tokens.dtype)
    far = pl.BlockSpec(memory_space=pltpu.HBM)
    return pl.pallas_call(
        kernel,
        out_shape=tuple(pltpu.HBM(shape.shape, shape.dtype) for shape in (out_shape, selector)),
        in_specs=[far, far, far],
        out_specs=(far, far),
        scratch_shapes=[
            pltpu.VMEM(choice.shape, choice.dtype),
            pltpu.VMEM((2, *tokens.shape), tokens.dtype),
            pltpu.VMEM(out_shape.shape, out_shape.dtype),
            pltpu.VMEM(selector.shape, selector.dtype),
            pltpu.SemaphoreType.DMA((6,)),
        ],
        compiler_params=pltpu.CompilerParams(vmem_limit_bytes=20 * 1024 * 1024),
    )(*(pltpu.with_memory_space_constraint(a, pltpu.HBM) for a in (choice, tokens, cotangent)))


def unpack_kernel(selector, back, outputs, input_grad, results, sems):
    lanes = back.shape[2]
    count = back.shape[1] // 2
    stores = []
    for number, target in enumerate((outputs, input_grad)):
        blocks = jnp.swapaxes(back[:, number * count : (number + 1) * count], 0, 1)
        for pair in range(0, count, 2):
            rows = jnp.concatenate([blocks[pair], blocks[pair + 1]], axis=1)
            results[number, :, pair * lanes : (pair + 2) * lanes] = contract_rows(
                selector[...], rows
            ).astype(results.dtype)
        stores.append(pltpu.make_async_copy(results.at[number], target, sems.at[number]))
        stores[-1].start()
    for store in stores:
        store.wait()


def exchange(rows, expert_count):
    row_count, blocks, lanes = rows.shape
    sent = rows.reshape(expert_count, row_count // expert_count * blocks, lanes)
    order = [
        (FIRST * PAIR - back) % expert_count + within
        for back in range(0, expert_count, PAIR)
        for within in range(PAIR)
    ]
    arrived = lax.all_to_all(
        sent, "ep", split_axis=0, concat_axis=0, tiled=True, axis_index_groups=[order]
    )
    return arrived.reshape(rows.shape)


Y, X_HI = 4, 2


def core_swap(array):
    return lax.ppermute(array, "fsdp", [(f, f ^ 1) for f in range(2 * Y * X_HI)])


def chip_shift(array, dy, dx):
    pairs = []
    for y in range(Y):
        for x in range(X_HI):
            for core in range(2):
                pairs.append(
                    ((y * X_HI + x) * 2 + core, ((y + dy) % Y * X_HI + (x ^ dx)) * 2 + core)
                )
    return lax.ppermute(array, "fsdp", pairs)


def chip_at(chip, dy, dx):
    return lax.bitwise_and(chip // X_HI + dy, Y - 1) * X_HI + lax.bitwise_xor(chip % X_HI, dx)


def gather_weights(shard, chip, core):
    across, two = chip_shift(shard, 0, 1), chip_shift(shard, 2, 0)
    one, three = chip_shift(shard, 1, 0), chip_shift(shard, 3, 0)
    early = [(shard, 0, 0), (one, 3, 0), (three, 1, 0), (chip_shift(across, 1, 0), 3, 1)]
    late = [(across, 0, 1), (two, 2, 0), (chip_shift(across, 3, 0), 1, 1), (chip_shift(two, 0, 1), 2, 1)]
    groups, numbers = [], []
    for parts in (early, late):
        held = jnp.concatenate([part for part, _, _ in parts], axis=0)
        for array, side in ((held, core), (core_swap(held), 1 - core)):
            groups.append(array)
            numbers += [chip_at(chip, dy, dx) * 2 + side for _, dy, dx in parts]
    return groups, jnp.stack(numbers).astype(jnp.int32)


def expert_kernel(numbers, arrived, *refs):
    groups, (back, sides_out, rows_out) = refs[:4], refs[4:7]
    x_rows, dy_rows, y_blocks, dx_blocks, y_back, dx_back, sides, pre, grad_hidden, sems = refs[7:]
    block = arrived.shape[2]
    blocks = arrived.shape[1] // 2
    hidden_width = sides.shape[1] // 3
    stores = []

    def store(source, target):
        stores.append(pltpu.make_async_copy(source, target, sems.at[len(stores)]))
        stores[-1].start()

    pairs = [
        group.at[pl.ds(start, 2 * block)]
        for group in groups
        for start in range(0, group.shape[0], 2 * block)
    ]

    def product(rows, columns, total):
        for place, weights in enumerate(pairs):
            both = [rows[numbers[2 * place + half]] for half in range(2)]
            part = jnp.dot(
                jnp.concatenate(both, axis=1),
                weights[:, columns],
                preferred_element_type=jnp.float32,
            )
            if place == 0:
                total[...] = part
            else:
                total[...] += part

    def back_product(left, columns, result):
        left = left.T
        for place, weights in enumerate(pairs):
            part = jnp.dot(weights[:, columns], left, preferred_element_type=jnp.float32)
            part = part.T.astype(result.dtype)
            for half in range(2):
                result[numbers[2 * place + half]] = part[:, half * block : (half + 1) * block]

    gate_up, down = slice(0, 2 * hidden_width), slice(2 * hidden_width, 3 * hidden_width)
    x_rows[...] = jnp.swapaxes(arrived[:, :blocks], 0, 1)
    store(x_rows, rows_out.at[pl.ds(0, blocks)])
    dy_rows[...] = jnp.swapaxes(arrived[:, blocks:], 0, 1)
    store(dy_rows, rows_out.at[pl.ds(blocks, blocks)])

    product(x_rows, gate_up, pre)
    product(dy_rows, down, grad_hidden)
    gate_pre = pre[:, :hidden_width]
    up_proj = pre[:, hidden_width:]
    upstream = grad_hidden[...]
    sigmoid_gate = jax.nn.sigmoid(gate_pre)
    activated = gate_pre * sigmoid_gate
    hidden = (activated * up_proj).astype(sides.dtype)
    sides[:, down] = hidden
    sides[:, :hidden_width] = (
        upstream * up_proj * sigmoid_gate * (1.0 + gate_pre * (1.0 - sigmoid_gate))
    ).astype(sides.dtype)
    sides[:, hidden_width : 2 * hidden_width] = (upstream * activated).astype(sides.dtype)
    store(sides, sides_out)

    back_product(hidden, down, y_blocks)
    y_back[...] = jnp.swapaxes(y_blocks[...], 0, 1)
    store(y_back, back.at[:, pl.ds(0, blocks)])
    back_product(sides[:, gate_up], gate_up, dx_blocks)
    step = back.shape[0] // 5
    for number in range(5):
        part = pl.ds(number * step, step)
        dx_back[part] = jnp.swapaxes(dx_blocks[:, part], 0, 1)
        store(dx_back.at[part], back.at[part, pl.ds(blocks, blocks)])
    for copy in stores:
        copy.wait()


def expert_rows(arrived, groups, numbers, hidden_width):
    row_count, blocks, lanes = arrived.shape
    return vmem_call(
        expert_kernel,
        (
            jax.ShapeDtypeStruct(arrived.shape, arrived.dtype),
            jax.ShapeDtypeStruct((row_count, 3 * hidden_width), arrived.dtype),
            jax.ShapeDtypeStruct((blocks, row_count, lanes), arrived.dtype),
        ),
        numbers,
        arrived,
        *groups,
        scratch_shapes=[
            *[pltpu.VMEM((blocks // 2, row_count, lanes), arrived.dtype)] * 4,
            *[pltpu.VMEM((row_count, blocks // 2, lanes), arrived.dtype)] * 2,
            pltpu.VMEM((row_count, 3 * hidden_width), arrived.dtype),
            pltpu.VMEM((row_count, 2 * hidden_width), jnp.float32),
            pltpu.VMEM((row_count, hidden_width), jnp.float32),
            pltpu.SemaphoreType.DMA((9,)),
        ],
        far_out=True,
    )


def terms_kernel(numbers, own, other, own_sides, other_sides, *terms):
    blocks = own.shape[0] // 2
    hidden_width = own_sides.shape[1] // 3
    for place, term in enumerate(terms):
        number = numbers[place]
        for first, sides in ((0, slice(0, 2 * hidden_width)), (blocks, slice(2 * hidden_width, None))):
            total = contract_rows(own[first + number], own_sides[:, sides])
            total += contract_rows(other[first + number], other_sides[:, sides])
            term[:, sides] = total.astype(term.dtype)


def local(tokens, cotangent, bucket, w_gate, w_up, w_down):
    token_count, model_width = tokens.shape
    expert_count = lax.axis_size("ep")
    capacity = max(2, 5 * token_count // (4 * expert_count))
    slot_rows = expert_count * capacity
    shard_width = w_gate.shape[1]
    hidden_width = w_gate.shape[2]
    place = lax.axis_index("fsdp")
    core = lax.bitwise_and(place, 1)
    chip = lax.shift_right_logical(place, 1)
    sizes = (expert_count, capacity)
    choice = bucket.reshape(1, token_count)

    blocked = jax.ShapeDtypeStruct(
        (slot_rows, 2 * model_width // shard_width, shard_width), tokens.dtype
    )
    packed, selector = pack_rows(functools.partial(pack_kernel, *sizes), blocked, choice, tokens, cotangent)
    packed, w_gate, w_up, w_down = lax.optimization_barrier((packed, w_gate, w_up, w_down))
    arrived = exchange(packed, expert_count)
    shard = jnp.concatenate([w_gate[0], w_up[0], w_down[0]], axis=1)
    groups, numbers = gather_weights(shard, chip, core)
    returned, sides, rows = expert_rows(arrived, groups, numbers, hidden_width)
    returned, rows, sides = lax.optimization_barrier((returned, rows, sides))
    back = exchange(returned, expert_count)

    other_rows = core_swap(rows)
    other_sides = core_swap(sides)
    targets = [(dy, dx) for dy in range(Y) for dx in range(X_HI)]
    columns = jnp.stack([chip_at(chip, dy, dx) * 2 + core for dy, dx in targets]).astype(jnp.int32)
    shape = jax.ShapeDtypeStruct((shard_width, 3 * hidden_width), tokens.dtype)
    terms = vmem_call(
        terms_kernel, [shape] * len(targets), columns, rows, other_rows, sides, other_sides
    )
    terms = dict(zip(targets, terms))

    def add(*arrays):
        return sum(array.astype(jnp.float32) for array in arrays)

    def summed(*arrays):
        return add(*arrays).astype(tokens.dtype)

    near, far = chip_shift(terms[1, 1], 1, 0), chip_shift(terms[3, 1], 3, 0)
    one, three = chip_shift(terms[1, 0], 1, 0), chip_shift(terms[3, 0], 3, 0)
    two = summed(terms[2, 0], chip_shift(terms[2, 1], 0, 1))
    across = summed(terms[0, 1], near, far)
    partial = add(terms[0, 0], one, three)
    last = add(chip_shift(two, 2, 0), chip_shift(across, 0, 1))
    last, partial = lax.optimization_barrier((last, partial))
    total = last + partial

    grads = total.astype(jnp.bfloat16)
    grad_wg = grads[None, :, :hidden_width]
    grad_wu = grads[None, :, hidden_width : 2 * hidden_width]
    grad_wd = grads[None, :, 2 * hidden_width :]
    result = jax.ShapeDtypeStruct(tokens.shape, tokens.dtype)
    outputs, input_grad = vmem_call(
        unpack_kernel,
        (result, result),
        None,
        selector,
        back,
        scratch_shapes=[
            pltpu.VMEM((2, *tokens.shape), tokens.dtype),
            pltpu.SemaphoreType.DMA((2,)),
        ],
        far_out=True,
    )
    return (outputs, input_grad, grad_wg, grad_wu, grad_wd)


def solution(mesh):
    in_specs = (
        P(("ep", "fsdp"), None),
        P(("ep", "fsdp"), None),
        P(("ep", "fsdp"), None),
        P("ep", "fsdp", None),
        P("ep", "fsdp", None),
        P("ep", "fsdp", None),
    )
    out_specs = (
        P(("ep", "fsdp"), None),
        P(("ep", "fsdp"), None),
        P("ep", "fsdp", None),
        P("ep", "fsdp", None),
        P("ep", "fsdp", None),
    )
    return jax.shard_map(local, mesh=mesh, in_specs=in_specs, out_specs=out_specs, check_vma=False)
```
